32 devices in a mesh: replica: 8 (over y, x, core), group: 4 (over z).
Axes of the slice: x: 2, y: 2, z: 4, core: 2. Of those that a mesh axis runs over, the one named last changes fastest.
Arguments:
- tokens: bfloat16 [8, 1024, 576], P('replica', 'group'), may hold values from -6 to 6
- segments: int32 [8, 1024], P('replica', 'group'), may hold values from 0 to 2, as said below
- positions: int32 [8, 1024], P('replica', 'group'), may hold values from 0 to 1278, as said below
- cotangent: bfloat16 [8, 1024, 576], P('replica', 'group'), may hold values from -6 to 6
- w_query: bfloat16 [2, 576, 576], P(None, 'group'), may hold values from -0.25 to 0.25
- key_weight: bfloat16 [2, 576, 192], P(None, 'group'), may hold values from -0.25 to 0.25
- value_weight: bfloat16 [2, 576, 192], P(None, 'group'), may hold values from -0.25 to 0.25
- w_out: bfloat16 [2, 576, 576], P(None, 'group'), may hold values from -1 to 1
- w_gate: bfloat16 [2, 576, 1536], P(None, 'group'), may hold values from -0.25 to 0.25
- w_up: bfloat16 [2, 576, 1536], P(None, 'group'), may hold values from -0.25 to 0.25
- w_down: bfloat16 [2, 1536, 576], P(None, 'group'), may hold values from -0.15625 to 0.15625
- norm_gains: float32 [2, 2, 576], replicated, may hold values from 0.1 to 1.9
Outputs:
- out: bfloat16 [8, 1024, 576], P('replica', 'group')
- grad_tokens: float32 [8, 1024, 576], P('replica', 'group')
- grad_w_query: float32 [2, 576, 576], P(None, 'group', 'replica')
- grad_w_key: float32 [2, 576, 192], P(None, 'group', 'replica')
- grad_w_value: float32 [2, 576, 192], P(None, 'group', 'replica')
- grad_w_out: float32 [2, 576, 576], P(None, 'group', 'replica')
- grad_w_gate: float32 [2, 576, 1536], P(None, 'group', 'replica')
- grad_w_up: float32 [2, 576, 1536], P(None, 'group', 'replica')
- grad_w_down: float32 [2, 1536, 576], P(None, 'group', 'replica')
- grad_gains: float32 [2, 2, 576], replicated
The draws below stay inside these ranges and needn't reach their ends.
Inputs may be any that keep to these rules, and one draw needn't show every extreme that they name: `segments`: within a sequence, segment numbers start at 0 and never fall; tokens with equal numbers form one document; a sequence holds at most three documents. Within a document, positions rise by one from token to token; the first document of each sequence starts at 0.
All inputs are finite; a program needn't handle non-finite values.
Results may differ from the reference program's by a relative error of at most 0.03.
Values may be sent and summed in bfloat16 or wider, within the bound.
No kernel may reach another device: no remote copies, remote signals or barrier semaphores. Data moves between devices by JAX's collectives and lax.ppermute only.
A program may use at most 192 MiB of HBM per device.

```python
import jax
import jax.numpy as jnp
from jax import lax

MODEL_DIM = 576
QUERY_HEADS = 9
KEY_VALUE_HEADS = 3
HEAD_DIM = 64
FF = 1536
DECODER_LAYERS = 2
LENGTH = 1024
SEQ_DEV = 1
STRETCH = 256
SEQS = 8
N_REPLICA = 8


def packing(key):
    key_breaks, key_span, key_opening, key_closing, key_offset = jax.random.split(key, 5)
    places = jnp.arange(LENGTH, dtype=jnp.int32)[None, :]
    breaks = jax.random.randint(key_breaks, (SEQS, LENGTH), 0, max(LENGTH // 3, 2)) == 0
    chosen = jax.random.randint(key_span, (N_REPLICA, 1), 0, SEQ_DEV)
    spanning = (jnp.arange(SEQ_DEV, dtype=jnp.int32)[None, :] == chosen).reshape(SEQS, 1)
    reach = max(STRETCH // 2, 2)
    opening = jax.random.randint(key_opening, (SEQS, 1), 1, reach)
    closing = LENGTH - jax.random.randint(key_closing, (SEQS, 1), 1, reach)
    span_breaks = (places == opening) | (places == closing)
    breaks = jnp.where(spanning, span_breaks, breaks)
    breaks = breaks & (places > 0)
    counted = jnp.cumsum(breaks.astype(jnp.int32), axis=1).astype(jnp.int32)
    breaks = breaks & (counted <= 2)
    segment_ids = jnp.cumsum(breaks.astype(jnp.int32), axis=1).astype(jnp.int32)
    starts = lax.cummax(jnp.where(breaks, places, 0).astype(jnp.int32), axis=1)
    offsets = jax.random.randint(key_offset, (SEQS, LENGTH), 0, 256)
    base = jnp.take_along_axis(offsets, starts, axis=1)
    top_offset = LENGTH + 254 - (closing - 1 - opening)
    base = jnp.where(spanning & (starts == opening), top_offset, base)
    base = jnp.where(starts == 0, 0, base)
    position_ids = places - starts + base
    return (segment_ids, position_ids.astype(jnp.int32))


def draw_segments(key, part):
    return packing(key)[0]


def draw_positions(key, part):
    return packing(key)[1]


def spiked(values, rng, source, target, parts, factor):
    def block_of(axis_at):
        return (jnp.arange(values.shape[axis_at]) // (values.shape[axis_at] // parts)).reshape((-1,) + (1,) * (values.ndim - 1 - axis_at))

    one_side = jax.random.permutation(rng, parts)[block_of(target)]
    second = (block_of(target) + parts // 2) % parts
    return jnp.where((block_of(source) == one_side) | (block_of(source) == second), factor * values, values)


def block_levels(stream_key, extent, shards, least, top_value):
    factor_of = 1.0
    for axis_at, shards_of in shards:
        draws = jax.random.uniform(jax.random.fold_in(jax.random.fold_in(stream_key, 6), axis_at), (shards_of,), jnp.float32, least / len(shards), top_value / len(shards))
        factor_of = factor_of * jnp.repeat(jnp.exp(draws), extent[axis_at] // shards_of).reshape((-1,) + (1,) * (len(extent) - 1 - axis_at))
    return factor_of


def normal_values(rng, extent, spread, bound, cuts=(), kind=jnp.bfloat16):
    values = spread * jax.random.normal(rng, extent, jnp.float32)
    if cuts:
        values = values * block_levels(rng, extent, cuts, -0.22, 0.18)
    return jnp.clip(values, -bound, bound).astype(kind)


def gaussian_with(own_key, shape, scale, most, cuts, heavy, held_as=jnp.bfloat16):
    values = scale * jax.random.normal(own_key, shape, jnp.float32)
    if cuts:
        values = values * block_levels(own_key, shape, cuts, -0.22, 0.18)
    return jnp.clip(spiked(values, jax.random.fold_in(own_key, 3), *heavy), -most, most).astype(held_as)


def setup_inputs(seed: int = 0) -> dict:
    streams_of = jax.random.split(jax.random.key(seed), 13)
    return {
        "tokens": normal_values(streams_of[0], (SEQS, LENGTH, MODEL_DIM), 1.0, 6.0, ((0, 8), (1, 4))),
        "segments": draw_segments(jax.random.fold_in(streams_of[12], 71), 0),
        "positions": draw_positions(jax.random.fold_in(streams_of[12], 71), 0),
        "cotangent": gaussian_with(streams_of[3], (SEQS, LENGTH, MODEL_DIM), 1.0, 6.0, ((0, 8), (1, 4)), (0, 2, 8, 2.0)),
        "w_query": normal_values(streams_of[4], (DECODER_LAYERS, MODEL_DIM, QUERY_HEADS * HEAD_DIM), MODEL_DIM ** -0.5, 0.25, ((1, 4),)),
        "key_weight": normal_values(streams_of[5], (DECODER_LAYERS, MODEL_DIM, KEY_VALUE_HEADS * HEAD_DIM), MODEL_DIM ** -0.5, 0.25, ((1, 4),)),
        "value_weight": normal_values(streams_of[6], (DECODER_LAYERS, MODEL_DIM, KEY_VALUE_HEADS * HEAD_DIM), MODEL_DIM ** -0.5, 0.25, ((1, 4),)),
        "w_out": normal_values(streams_of[7], (DECODER_LAYERS, QUERY_HEADS * HEAD_DIM, MODEL_DIM), (QUERY_HEADS * HEAD_DIM // 16) ** -0.5, 1.0, ((1, 4),)),
        "w_gate": normal_values(streams_of[8], (DECODER_LAYERS, MODEL_DIM, FF), MODEL_DIM ** -0.5, 0.25, ((1, 4),)),
        "w_up": normal_values(streams_of[9], (DECODER_LAYERS, MODEL_DIM, FF), MODEL_DIM ** -0.5, 0.25, ((1, 4),)),
        "w_down": normal_values(streams_of[10], (DECODER_LAYERS, FF, MODEL_DIM), FF ** -0.5, 0.15625, ((1, 4),)),
        "norm_gains": jnp.clip(1.0 + 0.18 * jax.random.normal(streams_of[11], (DECODER_LAYERS, 2, MODEL_DIM), jnp.float32), 0.1, 1.9),
    }


EPSILON = 1e-05
MASKED = -1e+30
HIGHEST = lax.Precision.HIGHEST

@jax.custom_vjp
def reduced_precision(v):
    return lax.optimization_barrier(v.astype(jnp.bfloat16)).astype(jnp.float32)

@jax.custom_vjp
def reduced_backward(v):
    return v

def low_keep(v):
    return (reduced_precision(v), None)

def low_pass(kept, grad):
    return (grad,)

def back_keep(v):
    return (v, None)

def back_low(kept, grad):
    return (reduced_precision(grad),)
reduced_precision.defvjp(low_keep, low_pass)
reduced_backward.defvjp(back_keep, back_low)

def rope_tables(positions, head_size):
    halfway = head_size // 2
    inverse_freq = jnp.power(10000.0, -jnp.arange(halfway, dtype=jnp.float32) * (2.0 / head_size))
    angles = positions.astype(jnp.float32)[..., None] * inverse_freq
    return (jnp.cos(angles), jnp.sin(angles))

def apply_rotary(values, cosine_table, sine_table):
    halfway = values.shape[-1] // 2
    leading = values[..., :halfway]
    trailing = values[..., halfway:]
    cos_heads = cosine_table[..., None, :]
    sin_heads = sine_table[..., None, :]
    return jnp.concatenate([leading * cos_heads - trailing * sin_heads, trailing * cos_heads + leading * sin_heads], axis=-1)

def rms_scale(values, gain_row):
    return values * lax.rsqrt(lax.optimization_barrier(jnp.mean(values * values, axis=-1, keepdims=True)) + EPSILON) * gain_row

def swiglu(gate_proj, up_proj):
    return gate_proj * jax.nn.sigmoid(gate_proj) * up_proj

def product(left_side, right_side):
    return jnp.einsum('bsd,df->bsf', left_side, right_side, precision=HIGHEST)

def attend_one(packed):
    grouped_queries, key_head_rows, value_head_rows, seg_row = packed
    scores = jnp.einsum('qhgd,khd->hgqk', grouped_queries, key_head_rows, precision=HIGHEST) * 0.125
    scores = reduced_backward(scores)
    places = jnp.arange(seg_row.shape[0])
    allowed = (seg_row[:, None] == seg_row[None, :]) & (places[:, None] >= places[None, :])
    scores = jnp.where(allowed[None, None], scores, MASKED)
    row_top = lax.optimization_barrier(jnp.max(scores, axis=-1, keepdims=True))
    raised = jnp.exp(scores - row_top)
    weights_soft = raised / lax.optimization_barrier(jnp.sum(raised, axis=-1, keepdims=True))
    return jnp.einsum('hgqk,khd->qhgd', reduced_precision(weights_soft), value_head_rows, precision=HIGHEST)

def layer_forward(stream, weights_now, gains_now, seg_rows, cosine_table, sine_table):
    w_query, key_weight, value_weight, w_out, w_gate, w_up, w_down = weights_now
    batch_extent, sequence_length, model_width = stream.shape
    normed = reduced_precision(rms_scale(stream, gains_now[0]))
    query_raw = reduced_backward(product(normed, w_query))
    projected_key = reduced_backward(product(normed, key_weight))
    projected_value = product(normed, value_weight)
    rotated_query = reduced_precision(apply_rotary(query_raw.reshape(batch_extent, sequence_length, QUERY_HEADS, HEAD_DIM), cosine_table, sine_table))
    rotated_key = reduced_precision(apply_rotary(projected_key.reshape(batch_extent, sequence_length, KEY_VALUE_HEADS, HEAD_DIM), cosine_table, sine_table))
    value_reduced = reduced_precision(reduced_backward(projected_value)).reshape(batch_extent, sequence_length, KEY_VALUE_HEADS, HEAD_DIM)
    grouped_queries = rotated_query.reshape(batch_extent, sequence_length, KEY_VALUE_HEADS, QUERY_HEADS // KEY_VALUE_HEADS, HEAD_DIM)
    attended = lax.map(jax.checkpoint(attend_one), (grouped_queries, rotated_key, value_reduced, seg_rows))
    attended = reduced_precision(reduced_backward(attended.reshape(batch_extent, sequence_length, QUERY_HEADS * HEAD_DIM)))
    middle = stream + reduced_backward(product(attended, w_out))
    normed_mid = reduced_precision(rms_scale(middle, gains_now[1]))
    gate_proj = reduced_backward(product(normed_mid, w_gate))
    up_proj = reduced_backward(product(normed_mid, w_up))
    hidden = reduced_precision(swiglu(gate_proj, up_proj))
    return middle + reduced_backward(product(hidden, w_down))

def reference(tokens, segments, positions, cotangent, w_query, key_weight, value_weight, w_out, w_gate, w_up, w_down, norm_gains):
    weights = tuple((matrix.astype(jnp.float32) for matrix in (w_query, key_weight, value_weight, w_out, w_gate, w_up, w_down)))
    block_size = 4 if SEQS % 4 == 0 else 1
    block_count = SEQS // block_size

    def to_blocks(array):
        return array.reshape((block_count, block_size) + array.shape[1:])

    def one_block(totals, inputs):
        block_tokens, block_segments, block_positions, block_cotangent = inputs
        cosine_table, sine_table = rope_tables(block_positions, HEAD_DIM)

        def forward(stream, weights_all, gains_all):
            for layer_index in range(DECODER_LAYERS):
                weights_now = tuple((matrix[layer_index] for matrix in weights_all))
                stream = layer_forward(stream, weights_now, gains_all[layer_index], block_segments, cosine_table, sine_table)
            return stream
        result, pullback = jax.vjp(forward, block_tokens.astype(jnp.float32), weights, norm_gains)
        grad_stream, grad_weights, grad_gain_part = pullback(block_cotangent.astype(jnp.float32))
        new_weights = tuple((total_part + new_part for total_part, new_part in zip(totals[0], grad_weights)))
        return ((new_weights, totals[1] + grad_gain_part), (result.astype(jnp.bfloat16), grad_stream))
    initial = (tuple((jnp.zeros(matrix.shape, jnp.float32) for matrix in weights)), jnp.zeros(norm_gains.shape, jnp.float32))
    totals, results = lax.scan(one_block, initial, (to_blocks(tokens), to_blocks(segments), to_blocks(positions), to_blocks(cotangent)))
    outputs, grad_inputs = results
    grad_weights, grad_gains = totals
    return (outputs.reshape(SEQS, LENGTH, MODEL_DIM), grad_inputs.reshape(SEQS, LENGTH, MODEL_DIM), grad_weights[0], grad_weights[1], grad_weights[2], grad_weights[3], grad_weights[4], grad_weights[5], grad_weights[6], grad_gains)
```

```python
import functools

import jax
import jax.numpy as jnp
from jax import lax
from jax.experimental import pallas as pl
from jax.experimental.pallas import tpu as pltpu
from jax.sharding import PartitionSpec as P

QUERY_HEADS = 9
KEY_VALUE_HEADS = 3
HEAD_DIM = 64
LAYERS = 2
EPSILON = 1e-05
MASKED = -1e30
BF = jnp.bfloat16
F32 = jnp.float32
BOTH = ("replica", "group")
VMEM_BYTES = 40 * 1024 * 1024


def mm(a, b):
    return lax.dot_general(a, b, (((1,), (0,)), ((), ())), preferred_element_type=F32)


def mm_t(a, b):
    return lax.dot_general(a, b, (((1,), (1,)), ((), ())), preferred_element_type=F32)


def flip(value):
    return value.astype(F32).T


def call(body, outs, scalars, args, scratch=(), flops=0, moved=0, name=None):
    vmem = pl.BlockSpec(memory_space=pltpu.VMEM)
    specs = [pl.BlockSpec(memory_space=pltpu.SMEM)] * len(scalars) + [vmem] * len(args)
    many = isinstance(outs, (list, tuple))
    return pl.pallas_call(
        body,
        out_shape=outs,
        in_specs=specs,
        out_specs=[vmem] * len(outs) if many else vmem,
        scratch_shapes=list(scratch),
        compiler_params=pltpu.CompilerParams(vmem_limit_bytes=VMEM_BYTES),
        cost_estimate=pl.CostEstimate(flops=flops, bytes_accessed=moved, transcendentals=0),
        name=name,
    )(*scalars, *args)


def sds(shape, dtype=BF):
    return jax.ShapeDtypeStruct(tuple(shape), dtype)


def rotate(value, cosine, signed_sine):
    lane = lax.broadcasted_iota(jnp.int32, value.shape, 1) % HEAD_DIM
    other = jnp.where(lane < HEAD_DIM // 2, pltpu.roll(value, 96, 1), pltpu.roll(value, 32, 1))
    return value * cosine + other * signed_sine


def qkv_body(x_ref, g_ref, w_ref, cos_ref, sin_ref, n_ref, q_ref, kv_ref):
    x = x_ref[...]
    scale = lax.rsqrt(jnp.mean(x * x, axis=-1, keepdims=True) + EPSILON)
    normed = (x * scale * g_ref[...]).astype(BF)
    n_ref[...] = normed
    raw = mm(normed, w_ref[...])
    cosine, sine = cos_ref[...], sin_ref[...]
    low = lax.broadcasted_iota(jnp.int32, cosine.shape, 1) < HEAD_DIM
    for tile in range(8):
        part = raw[:, 128 * tile : 128 * tile + 128]
        at = slice(128 * tile, 128 * tile + 128)
        if tile == 0:
            kv_ref[:, at] = rotate(part, cosine, sine).astype(BF)
        elif tile == 1:
            kv_ref[:, at] = jnp.where(low, rotate(part, cosine, sine), part).astype(BF)
        elif tile == 2:
            kv_ref[:, at] = part.astype(BF)
        else:
            q_ref[:, 128 * (tile - 3) : 128 * (tile - 2)] = (
                rotate(part, cosine, sine) * 0.125
            ).astype(BF)


def attend_body(pieces, *refs):
    q_ref = refs[0]
    kv_refs = refs[1 : 1 + pieces]
    bias_ref, x_ref, wo_ref, att_ref, lse_ref, mid_ref, k_buf, v_flip, q_flip, att_flip = refs[
        1 + pieces :
    ]
    tokens = q_ref.shape[0]
    half = KEY_VALUE_HEADS * HEAD_DIM
    for p in range(pieces):
        k_buf[p * tokens : (p + 1) * tokens, :] = kv_refs[p][:, :half]
        v_flip[:, p * tokens : (p + 1) * tokens] = flip(kv_refs[p][...])[half:].astype(BF)
    q_flip[...] = flip(q_ref[...]).astype(BF)
    for head in range(QUERY_HEADS):
        group = head // (QUERY_HEADS // KEY_VALUE_HEADS)
        at = slice(HEAD_DIM * head, HEAD_DIM * head + HEAD_DIM)
        kat = slice(HEAD_DIM * group, HEAD_DIM * group + HEAD_DIM)
        scores = mm(k_buf[:, kat], q_flip[at, :]) + bias_ref[...]
        top = jnp.max(scores, axis=0, keepdims=True)
        raised = jnp.exp(scores - top)
        total = jnp.sum(raised, axis=0, keepdims=True)
        out = mm(v_flip[kat, :], raised.astype(BF))
        att_flip[at, :] = out * (1.0 / total)
        lse_ref[head : head + 1, :] = top + jnp.log(total)
    attended = att_flip[...].T.astype(BF)
    att_ref[...] = attended
    mid_ref[...] = x_ref[...] + mm(attended, wo_ref[...])


def ffn_body(mid_ref, g_ref, wgu_ref, wd_ref, out_ref):
    mid = mid_ref[...]
    scale = lax.rsqrt(jnp.mean(mid * mid, axis=-1, keepdims=True) + EPSILON)
    normed = (mid * scale * g_ref[...]).astype(BF)
    gate = mm(normed, wgu_ref[0])
    up = mm(normed, wgu_ref[1])
    hidden = (gate * jax.nn.sigmoid(gate) * up).astype(BF)
    out_ref[...] = (mid + mm(hidden, wd_ref[...])).astype(out_ref.dtype)


def norm_back(value, gain, grad):
    scale = lax.rsqrt(jnp.mean(value * value, axis=-1, keepdims=True) + EPSILON)
    gained = grad * gain
    inner = jnp.mean(gained * value, axis=-1, keepdims=True)
    gain_grad = jnp.sum(grad * value * scale, axis=0, keepdims=True)
    return scale * gained - value * (scale * scale * scale * inner), gain_grad


def slots(custom, x_first):
    if not custom:
        return [(0, 0, None)]
    found = []
    for half in range(2):
        for slot in range(4):
            high, low = slot >> 1, slot & 1
            x_bit, y_bit = (high, low) if x_first else (low, high)
            found.append((half, slot, half + 2 * x_bit + 4 * y_bit))
    return found


def rows_of(idx_ref, xor, rows):
    if xor is None:
        return slice(None)
    return pl.ds(pl.multiple_of((idx_ref[0] ^ xor) * rows, 8), rows)


def ffn_back_body(
    custom, idx_ref, mid_ref, grad_ref, g_ref, wgu_ref, wd_ref, wo_ref, *refs
):
    count = 2 if custom else 1
    gu_refs, d_refs = refs[:count], refs[count : 2 * count]
    gmid_ref, ga_ref, gatt_ref, gain_ref = refs[2 * count : 2 * count + 4]
    branch_flip, gate_flip, up_flip = refs[2 * count + 4 :]
    parts = 8 if custom else 1
    mid, grad = mid_ref[...], grad_ref[...].astype(F32)
    gain = g_ref[...]
    scale = lax.rsqrt(jnp.mean(mid * mid, axis=-1, keepdims=True) + EPSILON)
    normed = (mid * scale * gain).astype(BF)
    gate = mm(normed, wgu_ref[0])
    up = mm(normed, wgu_ref[1])
    sig = jax.nn.sigmoid(gate)
    hidden = (gate * sig * up).astype(BF)
    branch = grad.astype(BF)
    branch_flip[...] = flip(branch)
    grad_hidden = mm_t(branch, wd_ref[...])
    grad_gate = (grad_hidden * up * sig * (1.0 + gate * (1.0 - sig))).astype(BF)
    grad_up = (grad_hidden * gate * sig).astype(BF)
    gate_flip[...] = flip(grad_gate)
    up_flip[...] = flip(grad_up)
    for half, slot, xor in slots(custom, False):
        rows = branch_flip.shape[0] // parts
        left = branch_flip[rows_of(idx_ref, xor, rows), :].astype(BF)
        d_refs[half][slot] = mm(left, hidden).astype(BF)
    for half, slot, xor in slots(custom, True):
        rows = gate_flip.shape[0] // parts
        at = rows_of(idx_ref, xor, rows)
        gu_refs[half][slot, :rows, :] = mm(gate_flip[at, :].astype(BF), normed).astype(BF)
        gu_refs[half][slot, rows:, :] = mm(up_flip[at, :].astype(BF), normed).astype(BF)
    grad_normed = mm_t(grad_gate, wgu_ref[0]) + mm_t(grad_up, wgu_ref[1])
    back, gain_grad = norm_back(mid, gain, grad_normed)
    grad_mid = grad + back
    gmid_ref[...] = grad_mid
    gain_ref[...] = gain_grad
    attn = grad_mid.astype(BF)
    ga_ref[...] = attn
    gatt_ref[...] = mm_t(attn, wo_ref[...]).astype(BF)


def attend_back_body(pieces, halves, *refs):
    q_ref = refs[0]
    kv_refs = refs[1 : 1 + pieces]
    bias_ref, lse_ref, att_ref, gatt_ref = refs[1 + pieces : 5 + pieces]
    dq_ref = refs[5 + pieces]
    dkv_refs = refs[6 + pieces : 6 + pieces + halves]
    kv_buf, k_flip, q_flip, g_flip, att_flip, dk_buf, dv_buf = refs[6 + pieces + halves :]
    tokens = q_ref.shape[0]
    half = KEY_VALUE_HEADS * HEAD_DIM
    for p in range(pieces):
        kv_buf[p * tokens : (p + 1) * tokens, :] = kv_refs[p][...]
        k_flip[:, p * tokens : (p + 1) * tokens] = flip(kv_refs[p][...])[:half].astype(BF)
    q_flip[...] = flip(q_ref[...]).astype(BF)
    g_flip[...] = flip(gatt_ref[...]).astype(BF)
    att_flip[...] = flip(att_ref[...])
    per = QUERY_HEADS // KEY_VALUE_HEADS
    for group in range(KEY_VALUE_HEADS):
        kat = slice(HEAD_DIM * group, HEAD_DIM * group + HEAD_DIM)
        vat = slice(half + HEAD_DIM * group, half + HEAD_DIM * group + HEAD_DIM)
        dk = dv = None
        for head in range(per * group, per * group + per):
            at = slice(HEAD_DIM * head, HEAD_DIM * head + HEAD_DIM)
            scores = mm(kv_buf[:, kat], q_flip[at, :]) + bias_ref[...]
            probs = jnp.exp(scores - lse_ref[head : head + 1, :])
            grad_probs = mm(kv_buf[:, vat], g_flip[at, :])
            row_dot = jnp.sum(
                g_flip[at, :].astype(F32) * att_flip[at, :], axis=0, keepdims=True
            )
            grad_scores = (probs * (grad_probs - row_dot)).astype(BF)
            dv_part = mm(probs.astype(BF), gatt_ref[:, at])
            dk_part = mm(grad_scores, q_ref[:, at])
            dv = dv_part if dv is None else dv + dv_part
            dk = dk_part if dk is None else dk + dk_part
            dq_ref[at, :] = mm(k_flip[kat, :], grad_scores) * 0.125
        dk_buf[:, kat] = dk
        dv_buf[:, kat] = dv
    rows = dk_buf.shape[0] // halves
    for h in range(halves):
        at = slice(h * rows, h * rows + rows)
        dkv_refs[h][:, :half] = dk_buf[at, :].astype(BF)
        dkv_refs[h][:, half:] = dv_buf[at, :].astype(BF)


def query_back_body(
    custom, idx_ref, dq_ref, cos_ref, sin_ref, w_ref, n_ref, ga_ref, att_ref, *refs
):
    count = 2 if custom else 1
    oq_refs, gn_ref = refs[:count], refs[count]
    turned, ga_flip = refs[count + 1 :]
    parts = 8 if custom else 1
    cosine, sine = cos_ref[...], sin_ref[...]
    mid = HEAD_DIM // 2
    for head in range(QUERY_HEADS):
        a = dq_ref[HEAD_DIM * head : HEAD_DIM * head + mid, :]
        b = dq_ref[HEAD_DIM * head + mid : HEAD_DIM * head + HEAD_DIM, :]
        turned[HEAD_DIM * head : HEAD_DIM * head + mid, :] = a * cosine + b * sine
        turned[HEAD_DIM * head + mid : HEAD_DIM * head + HEAD_DIM, :] = b * cosine - a * sine
    ga_flip[...] = flip(ga_ref[...])
    normed, attended = n_ref[...], att_ref[...]
    width = turned.shape[0]
    rows = width // parts
    for half, slot, xor in slots(custom, False):
        at = rows_of(idx_ref, xor, rows)
        oq_refs[half][slot, :rows, :] = mm(ga_flip[at, :].astype(BF), attended).astype(BF)
        oq_refs[half][slot, rows:, :] = mm(turned[at, :].astype(BF), normed).astype(BF)
    grad_query = turned[...].T.astype(BF)
    kv_width = 2 * KEY_VALUE_HEADS * HEAD_DIM
    gn_ref[...] = mm_t(grad_query, w_ref[:, kv_width : kv_width + width])


def kv_back_body(
    custom, idx_ref, dkv_ref, cos_ref, sin_ref, w_ref, n_ref, gn_ref, x_ref, gmid_ref, g_ref, *refs
):
    count = 2 if custom else 1
    kv_refs = refs[:count]
    grad_ref, gain_ref, kv_flip = refs[count : count + 3]
    parts = 8 if custom else 1
    dkv = dkv_ref[...].astype(F32)
    cosine, sine = cos_ref[...], -sin_ref[...]
    low = lax.broadcasted_iota(jnp.int32, cosine.shape, 1) < HEAD_DIM
    first = rotate(dkv[:, :128], cosine, sine)
    second = jnp.where(low, rotate(dkv[:, 128:256], cosine, sine), dkv[:, 128:256])
    grad_kv = jnp.concatenate([first, second, dkv[:, 256:]], axis=1)
    kv_flip[...] = grad_kv.T
    normed = n_ref[...]
    width = KEY_VALUE_HEADS * HEAD_DIM
    rows = width // parts
    for half, slot, xor in slots(custom, True):
        if xor is None:
            left = kv_flip[...]
        else:
            start = pl.multiple_of((idx_ref[0] ^ xor) * rows, 8)
            left = jnp.concatenate(
                [kv_flip[pl.ds(start, rows), :], kv_flip[pl.ds(width + start, rows), :]], axis=0
            )
        kv_refs[half][slot] = mm(left.astype(BF), normed).astype(BF)
    grad_normed = gn_ref[...] + mm_t(grad_kv.astype(BF), w_ref[:, : 2 * width])
    back, gain_grad = norm_back(x_ref[...], g_ref[...], grad_normed)
    grad_ref[...] = gmid_ref[...] + back
    gain_ref[...] = gain_grad


def source_of(idx_ref, x_first, f_bit, s_bit, k, group_size):
    chip = (idx_ref[0] >> 1) ^ ((f_bit + 2 * s_bit) if x_first else (2 * f_bit + s_bit))
    depth = lax.rem(idx_ref[1] - (k + 1) + group_size, group_size)
    return chip, depth


def place_all(refs, idx_ref, x_first, group_size, put):
    for combo, ref in enumerate(refs):
        s_bit, c_bit = combo & 1, combo >> 1
        core = (idx_ref[0] & 1) ^ c_bit
        for f_bit in range(2):
            for k in range(group_size - 1):
                chip, depth = source_of(idx_ref, x_first, f_bit, s_bit, k, group_size)
                put(chip, depth, core, ref[f_bit, k])


def attention_weights_body(x_first, group_size, idx_ref, own_ref, *refs):
    kvq_ref, o_ref, buf = refs[4:]
    rows, cols = own_ref.shape

    def put(chip, depth, core, piece):
        at = pl.multiple_of(depth * rows + core * (rows - piece.shape[0]), 16)
        buf[pl.ds(at, piece.shape[0]), pl.ds(pl.multiple_of(chip * (cols // 4), 128), cols // 4)] = piece

    place_all(refs[:4], idx_ref, x_first, group_size, put)
    buf[pl.ds(pl.multiple_of(idx_ref[1] * rows, 16), rows), :] = own_ref[...]
    width = o_ref.shape[1]
    used = cols - width
    kvq_ref[:, used // 128 * 128 :] = jnp.zeros_like(kvq_ref[:, used // 128 * 128 :])
    kvq_ref[:, :used] = buf[:, :used]
    o_ref[...] = buf[:, used:]


def gate_weights_body(x_first, group_size, idx_ref, gate_ref, up_ref, *refs):
    out_ref = refs[4]
    rows, cols = gate_ref.shape

    def put(chip, depth, core, piece):
        out_ref[
            core,
            pl.ds(pl.multiple_of(depth * rows, 16), rows),
            pl.ds(pl.multiple_of(chip * (cols // 4), 128), cols // 4),
        ] = piece

    place_all(refs[:4], idx_ref, x_first, group_size, put)
    own = pl.ds(pl.multiple_of(idx_ref[1] * rows, 16), rows)
    out_ref[0, own, :] = gate_ref[...]
    out_ref[1, own, :] = up_ref[...]


def down_weights_body(x_first, group_size, idx_ref, own_ref, *refs):
    out_ref = refs[4]
    rows = own_ref.shape[0]

    def put(chip, depth, core, piece):
        at = pl.multiple_of(depth * rows + (2 * chip + core) * (rows // 8), 16)
        out_ref[pl.ds(at, rows // 8), :] = piece

    place_all(refs[:4], idx_ref, x_first, group_size, put)
    out_ref[pl.ds(pl.multiple_of(idx_ref[1] * rows, 16), rows), :] = own_ref[...]


def xor_pairs(count, bits):
    return [(i, i ^ bits) for i in range(count)]


def spread(piece, x_first):
    replicas, groups = lax.axis_size("replica"), lax.axis_size("group")
    swap = lambda v, bits: lax.ppermute(v, "replica", xor_pairs(replicas, bits))
    first, second = (2, 4) if x_first else (4, 2)
    column = jnp.stack(
        [
            lax.ppermute(piece, "group", [(i, (i + k) % groups) for i in range(groups)])
            for k in range(1, groups)
        ]
    )
    pair = jnp.stack([column, swap(column, first)])
    other = swap(pair, second)
    return pair, other, swap(pair, 1), swap(other, 1)


def gather(value):
    return lax.all_gather(value, "group", axis=0, tiled=True)


def attention_weights(custom, idx, x_first, wq, wk, wv, wo):
    if not custom:
        pad = jnp.zeros((wq.shape[0], 64), BF)
        return gather(jnp.concatenate([wk, wv, wq, pad], axis=1)), gather(wo)
    groups = lax.axis_size("group")
    unit = jnp.concatenate([wk, wv, wq, wo], axis=1)
    rows, cols = unit.shape
    piece = lax.dynamic_slice(
        unit, (64 * (idx[0] & 1), (idx[0] >> 1) * (cols // 4)), (rows - 64, cols // 4)
    )
    arrived = spread(piece, x_first)
    return call(
        functools.partial(attention_weights_body, x_first, groups),
        [sds((rows * groups, 1024)), sds((rows * groups, wo.shape[1]))],
        [idx],
        [unit, *arrived],
        [pltpu.VMEM((rows * groups, cols), BF)],
        moved=4000000,
        name="place_attention_weights",
    )


def gate_weights(custom, idx, x_first, wg, wu):
    if not custom:
        return jnp.stack([gather(wg), gather(wu)])
    groups = lax.axis_size("group")
    rows, cols = wg.shape
    at = (0, (idx[0] >> 1) * (cols // 4))
    piece = jnp.where(
        (idx[0] & 1) == 0,
        lax.dynamic_slice(wg, at, (rows, cols // 4)),
        lax.dynamic_slice(wu, at, (rows, cols // 4)),
    )
    arrived = spread(piece, x_first)
    return call(
        functools.partial(gate_weights_body, x_first, groups),
        sds((2, rows * groups, cols)),
        [idx],
        [wg, wu, *arrived],
        moved=7000000,
        name="place_gate_weights",
    )


def down_weights(custom, idx, x_first, wd):
    if not custom:
        return gather(wd)
    groups = lax.axis_size("group")
    rows, cols = wd.shape
    piece = lax.dynamic_slice(wd, (idx[0] * (rows // 8), 0), (rows // 8, cols))
    arrived = spread(piece, x_first)
    return call(
        functools.partial(down_weights_body, x_first, groups),
        sds((rows * groups, cols)),
        [idx],
        [wd, *arrived],
        moved=3500000,
        name="place_down_weights",
    )


def plus(a, b):
    return (a.astype(F32) + b.astype(F32)).astype(BF)


def reduce_rows(halves, x_first, width):
    replicas, groups = lax.axis_size("replica"), lax.axis_size("group")
    z = lax.axis_index("group")
    swap = lambda v, bits: lax.ppermute(v, "replica", xor_pairs(replicas, bits))
    first, second = (2, 4) if x_first else (4, 2)
    keep, send = halves
    got = swap(send, 1)
    low, high = plus(keep[:2], got[:2]), plus(keep[2:], got[2:])
    got = swap(high, first)
    mine, high = plus(low[0], got[0]), plus(low[1], got[1])
    mine = plus(mine, swap(high, second))
    cut = lambda k: lax.dynamic_slice_in_dim(mine, lax.rem(z + k, groups) * width, width, axis=1)
    total = cut(0).astype(F32)
    for k in range(1, groups):
        moved = lax.ppermute(cut(k), "group", [(i, (i + k) % groups) for i in range(groups)])
        total = total + moved.astype(F32)
    return total


def scatter_plain(value):
    part = lax.psum_scatter(value, "replica", scatter_dimension=1, tiled=True)
    return lax.psum_scatter(part, "group", scatter_dimension=0, tiled=True).astype(F32)


def sum_all(custom, value):
    if not custom:
        return lax.psum(value, BOTH)
    for bits in (1, 2, 4):
        value = value + lax.ppermute(value, "replica", xor_pairs(lax.axis_size("replica"), bits))
    for bits in (1, 2):
        value = value + lax.ppermute(value, "group", xor_pairs(lax.axis_size("group"), bits))
    return value


def local(
    tokens,
    segments,
    positions,
    cotangent,
    w_query,
    key_weight,
    value_weight,
    w_out,
    w_gate,
    w_up,
    w_down,
    norm_gains,
):
    sequences, length, width = tokens.shape
    replicas, groups = lax.axis_size("replica"), lax.axis_size("group")
    r, z = lax.axis_index("replica"), lax.axis_index("group")
    custom = replicas == 8 and groups == 4
    idx = jnp.stack([r, z]).astype(jnp.int32)
    hidden_width = w_gate.shape[2]
    kv_width = key_weight.shape[2]
    full = length * groups
    core_pairs = xor_pairs(replicas, 1)
    z_pairs = xor_pairs(groups, 1)

    half_way = groups // 2
    exchange = []
    for i in range(replicas):
        for j in range(groups):
            if i % 2 == 1 and j < half_way:
                target = (i - 1, j + half_way)
            elif i % 2 == 0 and j >= half_way:
                target = (i + 1, j - half_way)
            else:
                target = (i, j)
            exchange.append((i * groups + j, target[0] * groups + target[1]))

    def relocate(value):
        return lax.ppermute(value, BOTH, exchange) if custom else value

    def share(value):
        if not custom:
            every = lax.all_gather(value, "group", axis=0, tiled=False)
            return [every[i] for i in range(groups)]
        deep = lax.ppermute(value, "group", z_pairs)
        return [
            value,
            deep,
            lax.ppermute(value, "replica", core_pairs),
            lax.ppermute(deep, "replica", core_pairs),
        ]

    tokens = relocate(tokens.reshape(length, width))
    labels = relocate(jnp.stack([segments.reshape(length), positions.reshape(length)]))
    cotangent = relocate(cotangent.reshape(length, width))
    seg, pos = labels[0], labels[1]
    seg_all = jnp.concatenate(share(seg))
    if custom:
        block_at = lambda c, zz: c * half_way + zz % half_way
        c = r & 1
        blocks = [
            block_at(c, z),
            block_at(c, z ^ 1),
            block_at(c ^ 1, z),
            block_at(c ^ 1, z ^ 1),
        ]
    else:
        blocks = list(range(groups))
    mine_block = blocks[0] if custom else z
    ramp = jnp.arange(length, dtype=jnp.int32)
    place_all_keys = jnp.concatenate([b * length + ramp for b in blocks])
    place = mine_block * length + ramp
    allowed = (seg_all[:, None] == seg[None, :]) & (place_all_keys[:, None] <= place[None, :])
    bias = jnp.where(allowed, 0.0, MASKED).astype(F32)

    half_head = HEAD_DIM // 2
    inverse_freq = jnp.power(
        10000.0, -jnp.arange(half_head, dtype=F32) * (2.0 / HEAD_DIM)
    )
    angles = pos.astype(F32)[:, None] * inverse_freq
    cosine, sine = jnp.cos(angles), jnp.sin(angles)
    cos_wide = jnp.concatenate([cosine] * 4, axis=1)
    sin_wide = jnp.concatenate([-sine, sine] * 2, axis=1)
    cos_flip, sin_flip = cosine.T, sine.T

    orders = [(True, True, False), (False, False, True)]
    weights = []
    for layer in range(LAYERS):
        a_order, g_order, d_order = orders[layer]
        kvq, wo = attention_weights(
            custom, idx, a_order, w_query[layer], key_weight[layer], value_weight[layer], w_out[layer]
        )
        gu = gate_weights(custom, idx, g_order, w_gate[layer], w_up[layer])
        down = down_weights(custom, idx, d_order, w_down[layer])
        weights.append((kvq, wo, gu, down))

    tok_f32 = sds((length, width), F32)
    stream = tokens.astype(F32)
    kept = []
    att_flops = 4 * QUERY_HEADS * HEAD_DIM * length * full
    ffn_flops = 6 * length * width * hidden_width
    for layer in range(LAYERS):
        kvq, wo, gu, down = weights[layer]
        gains = norm_gains[layer]
        normed, q, kv = call(
            qkv_body,
            [sds((length, width)), sds((length, 640)), sds((length, 2 * kv_width))],
            [],
            [stream, gains[0:1], kvq, cos_wide, sin_wide],
            flops=2 * length * width * 1024,
            moved=2000000,
            name="project",
        )
        pieces = share(kv)
        attended, lse, middle = call(
            functools.partial(attend_body, groups),
            [sds((length, width)), sds((16, length), F32), tok_f32],
            [],
            [q, *pieces, bias, stream, wo],
            [
                pltpu.VMEM((full, kv_width), BF),
                pltpu.VMEM((kv_width, full), BF),
                pltpu.VMEM((640, length), BF),
                pltpu.VMEM((width, length), F32),
            ],
            flops=4 * att_flops,
            moved=4000000,
            name="attend",
        )
        after = call(
            ffn_body,
            sds((length, width), F32 if layer + 1 < LAYERS else BF),
            [],
            [middle, gains[1:2], gu, down],
            flops=ffn_flops,
            moved=7000000,
            name="feed_forward",
        )
        kept.append((stream, normed, q, pieces, lse, attended, middle))
        stream = after
    result = relocate(stream)

    grad = cotangent
    parts = 8 if custom else 1
    count = 2 if custom else 1
    slots_here = parts // count
    owned = [None] * LAYERS
    gain_rows = [None] * LAYERS
    for layer in reversed(range(LAYERS)):
        kvq, wo, gu, down = weights[layer]
        entry, normed, q, pieces, lse, attended, middle = kept[layer]
        gains = norm_gains[layer]

        def blocks_of(rows, cols):
            return [sds((slots_here, rows // parts, cols))] * count

        outs = call(
            functools.partial(ffn_back_body, custom),
            blocks_of(2 * hidden_width, width)
            + blocks_of(width, hidden_width)
            + [tok_f32, sds((length, width)), sds((length, width)), sds((1, width), F32)],
            [idx],
            [middle, grad, gains[1:2], gu, down, wo],
            [
                pltpu.VMEM((width, length), F32),
                pltpu.VMEM((hidden_width, length), F32),
                pltpu.VMEM((hidden_width, length), F32),
            ],
            flops=3 * ffn_flops,
            moved=16000000,
            name="feed_forward_back",
        )
        gu_parts, d_parts = outs[:count], outs[count : 2 * count]
        grad_mid, grad_attn, grad_att, gain_mid = outs[2 * count :]
        halves = 2 if custom else 1
        outs = call(
            functools.partial(attend_back_body, groups, halves),
            [sds((width, length), F32)] + [sds((full // halves, 2 * kv_width))] * halves,
            [],
            [q, *pieces, bias, lse, attended, grad_att],
            [
                pltpu.VMEM((full, 2 * kv_width), BF),
                pltpu.VMEM((kv_width, full), BF),
                pltpu.VMEM((640, length), BF),
                pltpu.VMEM((width, length), BF),
                pltpu.VMEM((width, length), F32),
                pltpu.VMEM((full, kv_width), F32),
                pltpu.VMEM((full, kv_width), F32),
            ],
            flops=10 * att_flops,
            moved=6000000,
            name="attend_back",
        )
        dq_flip, dkv = outs[0], outs[1:]
        if custom:
            got = lax.ppermute(dkv[1], "replica", core_pairs)
            deep = plus(dkv[0][length:], got[length:])
            near = dkv[0][:length].astype(F32) + got[:length].astype(F32)
            dkv_sum = near + lax.ppermute(deep, "group", z_pairs).astype(F32)
        else:
            dkv_sum = lax.psum_scatter(dkv[0], "group", scatter_dimension=0, tiled=True).astype(F32)
        dkv_sum = dkv_sum.astype(F32)
        outs = call(
            functools.partial(query_back_body, custom),
            blocks_of(2 * width, width) + [tok_f32],
            [idx],
            [dq_flip, cos_flip, sin_flip, kvq, normed, grad_attn, attended],
            [pltpu.VMEM((width, length), F32), pltpu.VMEM((width, length), F32)],
            flops=6 * length * width * width,
            moved=6000000,
            name="query_back",
        )
        oq_parts, grad_normed = outs[:count], outs[count]
        outs = call(
            functools.partial(kv_back_body, custom),
            blocks_of(2 * kv_width, width) + [tok_f32, sds((1, width), F32)],
            [idx],
            [dkv_sum, cos_wide, sin_wide, kvq, normed, grad_normed, entry, grad_mid, gains[0:1]],
            [pltpu.VMEM((2 * kv_width, length), F32)],
            flops=8 * length * width * kv_width,
            moved=5000000,
            name="key_value_back",
        )
        kv_parts, grad, gain_in = outs[:count], outs[count], outs[count + 1]
        gain_rows[layer] = jnp.concatenate([gain_in, gain_mid])
        if custom:
            cols = width // groups
            gu_own = reduce_rows(gu_parts, True, cols)
            d_own = reduce_rows(d_parts, False, hidden_width // groups)
            oq_own = reduce_rows(oq_parts, False, cols)
            kv_own = reduce_rows(kv_parts, True, cols)
            n_gate, n_out, n_key = hidden_width // 8, width // 8, kv_width // 8
            owned[layer] = (
                oq_own[n_out:].T,
                kv_own[:n_key].T,
                kv_own[n_key:].T,
                oq_own[:n_out].T,
                gu_own[:n_gate].T,
                gu_own[n_gate:].T,
                d_own.T,
            )
        else:
            gu_all, oq_all, kv_all = gu_parts[0][0], oq_parts[0][0], kv_parts[0][0]
            owned[layer] = tuple(
                scatter_plain(v.T)
                for v in (
                    oq_all[width:],
                    kv_all[:kv_width],
                    kv_all[kv_width:],
                    oq_all[:width],
                    gu_all[:hidden_width],
                    gu_all[hidden_width:],
                    d_parts[0][0],
                )
            )
    stacked = [jnp.stack([owned[layer][i] for layer in range(LAYERS)]) for i in range(7)]
    gain_total = sum_all(custom, jnp.stack(gain_rows).reshape(2 * LAYERS, width))
    grad_tokens = relocate(grad)
    return (
        result.reshape(sequences, length, width),
        grad_tokens.reshape(sequences, length, width),
        *stacked,
        gain_total.reshape(LAYERS, 2, width),
    )


def solution(mesh):
    sequence = P("replica", "group", None)
    matrix = P(None, "group", None)
    owner = P(None, "group", "replica")
    return jax.shard_map(
        local,
        mesh=mesh,
        in_specs=(sequence, P("replica", "group"), P("replica", "group"), sequence)
        + (matrix,) * 7
        + (P(),),
        out_specs=(sequence, sequence) + (owner,) * 7 + (P(),),
        check_vma=False,
    )
```

```python
import functools

import jax
import jax.numpy as jnp
from jax import lax
from jax.experimental import pallas as pl
from jax.experimental.pallas import tpu as pltpu
from jax.sharding import PartitionSpec as P

QUERY_HEADS = 9
KEY_VALUE_HEADS = 3
HEAD_DIM = 64
LAYERS = 2
EPSILON = 1e-05
MASKED = -1e30
BF = jnp.bfloat16
F32 = jnp.float32
BOTH = ("replica", "group")


def mm(a, b):
    return lax.dot_general(a, b, (((1,), (0,)), ((), ())), preferred_element_type=F32)


def mm_t(a, b):
    return lax.dot_general(a, b, (((1,), (1,)), ((), ())), preferred_element_type=F32)


def flip(value):
    return value.astype(F32).T


def call(
    body, outs, scalars, args, scratch=(), flops=0, moved=0, name=None, after=(), limit=32
):
    vmem = pl.BlockSpec(memory_space=pltpu.VMEM)
    specs = [pl.BlockSpec(memory_space=pltpu.SMEM)] * len(scalars) + [vmem] * len(args)
    specs += [pl.BlockSpec(memory_space=pl.ANY)] * len(after)
    many = isinstance(outs, (list, tuple))
    return pl.pallas_call(
        body,
        out_shape=outs,
        in_specs=specs,
        out_specs=[vmem] * len(outs) if many else vmem,
        scratch_shapes=list(scratch),
        compiler_params=pltpu.CompilerParams(vmem_limit_bytes=limit * 1024 * 1024),
        cost_estimate=pl.CostEstimate(flops=flops, bytes_accessed=moved, transcendentals=0),
        name=name,
    )(*scalars, *args, *after)


def sds(shape, dtype=BF):
    return jax.ShapeDtypeStruct(tuple(shape), dtype)


def rotate(value, cosine, signed_sine):
    lane = lax.broadcasted_iota(jnp.int32, value.shape, 1) % HEAD_DIM
    other = jnp.where(lane < HEAD_DIM // 2, pltpu.roll(value, 96, 1), pltpu.roll(value, 32, 1))
    return value * cosine + other * signed_sine


def qkv_body(x_ref, g_ref, w_ref, cos_ref, sin_ref, n_ref, q_ref, kv_ref):
    x = x_ref[...]
    scale = lax.rsqrt(jnp.mean(x * x, axis=-1, keepdims=True) + EPSILON)
    normed = (x * scale * g_ref[...]).astype(BF)
    n_ref[...] = normed
    raw = mm(normed, w_ref[...])
    cosine, sine = cos_ref[...], sin_ref[...]
    low = lax.broadcasted_iota(jnp.int32, cosine.shape, 1) < HEAD_DIM
    for tile in range(8):
        part = raw[:, 128 * tile : 128 * tile + 128]
        at = slice(128 * tile, 128 * tile + 128)
        if tile == 0:
            kv_ref[:, at] = rotate(part, cosine, sine).astype(BF)
        elif tile == 1:
            kv_ref[:, at] = jnp.where(low, rotate(part, cosine, sine), part).astype(BF)
        elif tile == 2:
            kv_ref[:, at] = part.astype(BF)
        else:
            q_ref[:, 128 * (tile - 3) : 128 * (tile - 2)] = (
                rotate(part, cosine, sine) * 0.125
            ).astype(BF)


def attend_body(pieces, *refs):
    q_ref = refs[0]
    kv_refs = refs[1 : 1 + pieces]
    bias_ref, x_ref, wo_ref, att_ref, lse_ref, mid_ref, k_buf, v_flip, q_flip, att_flip = refs[
        1 + pieces :
    ]
    tokens = q_ref.shape[0]
    half = KEY_VALUE_HEADS * HEAD_DIM
    for p in range(pieces):
        k_buf[p * tokens : (p + 1) * tokens, :] = kv_refs[p][:, :half]
        v_flip[:, p * tokens : (p + 1) * tokens] = flip(kv_refs[p][...])[half:].astype(BF)
    q_flip[...] = flip(q_ref[...]).astype(BF)
    for head in range(QUERY_HEADS):
        group = head // (QUERY_HEADS // KEY_VALUE_HEADS)
        at = slice(HEAD_DIM * head, HEAD_DIM * head + HEAD_DIM)
        kat = slice(HEAD_DIM * group, HEAD_DIM * group + HEAD_DIM)
        scores = mm(k_buf[:, kat], q_flip[at, :]) + bias_ref[...]
        top = jnp.max(scores, axis=0, keepdims=True)
        raised = jnp.exp(scores - top)
        total = jnp.sum(raised, axis=0, keepdims=True)
        out = mm(v_flip[kat, :], raised.astype(BF))
        att_flip[at, :] = out * (1.0 / total)
        lse_ref[head : head + 1, :] = top + jnp.log(total)
    attended = att_flip[...].T.astype(BF)
    att_ref[...] = attended
    mid_ref[...] = x_ref[...] + mm(attended, wo_ref[...])


def ffn_body(mid_ref, g_ref, wgu_ref, wd_ref, out_ref):
    mid = mid_ref[...]
    scale = lax.rsqrt(jnp.mean(mid * mid, axis=-1, keepdims=True) + EPSILON)
    normed = (mid * scale * g_ref[...]).astype(BF)
    gate = mm(normed, wgu_ref[0])
    up = mm(normed, wgu_ref[1])
    hidden = (gate * jax.nn.sigmoid(gate) * up).astype(BF)
    out_ref[...] = (mid + mm(hidden, wd_ref[...])).astype(out_ref.dtype)


def norm_back(value, gain, grad):
    scale = lax.rsqrt(jnp.mean(value * value, axis=-1, keepdims=True) + EPSILON)
    gained = grad * gain
    inner = jnp.mean(gained * value, axis=-1, keepdims=True)
    gain_grad = jnp.sum(grad * value * scale, axis=0, keepdims=True)
    return scale * gained - value * (scale * scale * scale * inner), gain_grad


def slots(custom, x_first):
    if not custom:
        return [(0, 0, None)]
    found = []
    for half in range(2):
        for slot in range(4):
            high, low = slot >> 1, slot & 1
            x_bit, y_bit = (high, low) if x_first else (low, high)
            found.append((half, slot, half + 2 * x_bit + 4 * y_bit))
    return found


def rows_of(idx_ref, xor, rows):
    if xor is None:
        return slice(None)
    return pl.ds(pl.multiple_of((idx_ref[0] ^ xor) * rows, 8), rows)


def by_depth(custom, idx_ref, count, size):
    if not custom:
        return [slice(None)]
    order = [(t & 1) * 2 + (t >> 1) for t in range(count)]
    return [pl.ds(pl.multiple_of((idx_ref[1] ^ t) * size, size & -size), size) for t in order]


def fold(refs, outs):
    for i in range(0, len(refs), 2):
        count = refs[i].shape[0] // 2
        for half in range(2):
            at = slice(half * count, half * count + count)
            total = refs[i][at].astype(F32) + refs[i + 1][at].astype(F32)
            outs[i + half][...] = total.astype(BF)


def step_body(folds, gained, *refs):
    ins = 2 * folds + 2 * gained
    fold(refs[: 2 * folds], refs[ins : ins + 2 * folds])
    if gained:
        refs[-1][...] = refs[2 * folds][...] + refs[2 * folds + 1][...]


def ffn_back_body(custom, groups, last, idx_ref, *refs):
    mid_ref, grad_ref, g_ref, gu_ref, wd_ref, wo_ref, att_ref = refs[:7]
    refs = refs[7:]
    count = 2 if custom else 1
    a_refs, b_refs = refs[:count], refs[count : 2 * count]
    gmid_ref, gatt_ref, gain_ref = refs[2 * count : 2 * count + 3]
    refs = refs[2 * count + 3 :]
    if last:
        result_ref, refs = refs[0], refs[1:]
    branch_flip, gate_flip, up_flip, flat, deep_flip, hidden_buf, hidden_deep = refs
    parts = 8 if custom else 1
    depths = groups if custom else 1
    mid, grad = mid_ref[...], grad_ref[...].astype(F32)
    gain = g_ref[...]
    width, hidden_width = branch_flip.shape[0], gate_flip.shape[0]
    cut, hidden_cut = width // depths, hidden_width // depths
    scale = lax.rsqrt(jnp.mean(mid * mid, axis=-1, keepdims=True) + EPSILON)
    normed = (mid * scale * gain).astype(BF)
    gate = mm(normed, gu_ref[0])
    up = mm(normed, gu_ref[1])
    sig = jax.nn.sigmoid(gate)
    hidden_buf[...] = (gate * sig * up).astype(BF)
    if last:
        result_ref[...] = (mid + mm(hidden_buf[...], wd_ref[...])).astype(BF)
    branch = grad.astype(BF)
    branch_flip[...] = flip(branch)
    grad_hidden = mm_t(branch, wd_ref[...])
    grad_gate = (grad_hidden * up * sig * (1.0 + gate * (1.0 - sig))).astype(BF)
    grad_up = (grad_hidden * gate * sig).astype(BF)
    grad_normed = mm_t(grad_gate, gu_ref[0]) + mm_t(grad_up, gu_ref[1])
    back, gain_grad = norm_back(mid, gain, grad_normed)
    grad_mid = grad + back
    gmid_ref[...] = grad_mid
    gain_ref[...] = gain_grad
    attn = grad_mid.astype(BF)
    gatt_ref[...] = mm_t(attn, wo_ref[...]).astype(BF)
    gate_flip[...] = flip(grad_gate).astype(BF)
    up_flip[...] = flip(grad_up).astype(BF)
    flat[...] = flip(normed)
    for t, at in enumerate(by_depth(custom, idx_ref, depths, cut)):
        deep_flip[t * cut : t * cut + cut, :] = flat[at, :].astype(BF)
    rows = hidden_width // parts
    for half, slot, xor in slots(custom, True):
        at = rows_of(idx_ref, xor, rows)
        right = jnp.concatenate([gate_flip[at, :], up_flip[at, :]], axis=0)
        block = mm_t(deep_flip[...], right).astype(BF)
        for t in range(depths):
            a_refs[half][slot * depths + t] = block[t * cut : t * cut + cut]
    for t, at in enumerate(by_depth(custom, idx_ref, depths, hidden_cut)):
        hidden_deep[:, t * hidden_cut : t * hidden_cut + hidden_cut] = hidden_buf[:, at]
    rows = width // parts
    for half, slot, xor in slots(custom, False):
        left = branch_flip[rows_of(idx_ref, xor, rows), :].astype(BF)
        block = mm(left, hidden_deep[...]).astype(BF)
        for t in range(depths):
            b_refs[half][slot * depths + t, :, :hidden_cut] = block[
                :, t * hidden_cut : t * hidden_cut + hidden_cut
            ]
    flat[...] = flip(att_ref[...])
    for t, at in enumerate(by_depth(custom, idx_ref, depths, cut)):
        deep_flip[t * cut : t * cut + cut, :] = flat[at, :].astype(BF)
    branch_flip[...] = flip(attn)
    for half, slot, xor in slots(custom, False):
        left = branch_flip[rows_of(idx_ref, xor, rows), :].astype(BF)
        block = mm_t(left, deep_flip[...]).astype(BF)
        for t in range(depths):
            b_refs[half][slot * depths + t, :, hidden_cut:] = block[:, t * cut : t * cut + cut]


def attend_back_body(pieces, halves, folds, *refs):
    q_ref = refs[0]
    kv_refs = refs[1 : 1 + pieces]
    bias_ref, lse_ref, att_ref, gatt_ref = refs[1 + pieces : 5 + pieces]
    old = refs[5 + pieces : 5 + pieces + 2 * folds]
    refs = refs[5 + pieces + 2 * folds :]
    dq_ref, dkv_refs = refs[0], refs[1 : 1 + halves]
    fold(old, refs[1 + halves : 1 + halves + 2 * folds])
    kv_buf, k_flip, q_flip, g_flip, att_flip, dk_buf, dv_buf = refs[1 + halves + 2 * folds :]
    tokens = q_ref.shape[0]
    half = KEY_VALUE_HEADS * HEAD_DIM
    for p in range(pieces):
        kv_buf[p * tokens : (p + 1) * tokens, :] = kv_refs[p][...]
        k_flip[:, p * tokens : (p + 1) * tokens] = flip(kv_refs[p][...])[:half].astype(BF)
    q_flip[...] = flip(q_ref[...]).astype(BF)
    g_flip[...] = flip(gatt_ref[...]).astype(BF)
    att_flip[...] = flip(att_ref[...])
    per = QUERY_HEADS // KEY_VALUE_HEADS
    for group in range(KEY_VALUE_HEADS):
        kat = slice(HEAD_DIM * group, HEAD_DIM * group + HEAD_DIM)
        vat = slice(half + HEAD_DIM * group, half + HEAD_DIM * group + HEAD_DIM)
        dk = dv = None
        for head in range(per * group, per * group + per):
            at = slice(HEAD_DIM * head, HEAD_DIM * head + HEAD_DIM)
            scores = mm(kv_buf[:, kat], q_flip[at, :]) + bias_ref[...]
            probs = jnp.exp(scores - lse_ref[head : head + 1, :])
            grad_probs = mm(kv_buf[:, vat], g_flip[at, :])
            row_dot = jnp.sum(
                g_flip[at, :].astype(F32) * att_flip[at, :], axis=0, keepdims=True
            )
            grad_scores = (probs * (grad_probs - row_dot)).astype(BF)
            dv_part = mm(probs.astype(BF), gatt_ref[:, at])
            dk_part = mm(grad_scores, q_ref[:, at])
            dv = dv_part if dv is None else dv + dv_part
            dk = dk_part if dk is None else dk + dk_part
            dq_ref[at, :] = mm(k_flip[kat, :], grad_scores) * 0.125
        dk_buf[:, kat] = dk
        dv_buf[:, kat] = dv
    rows = dk_buf.shape[0] // halves
    for h in range(halves):
        at = slice(h * rows, h * rows + rows)
        dkv_refs[h][:, :half] = dk_buf[at, :].astype(BF)
        dkv_refs[h][:, half:] = dv_buf[at, :].astype(BF)


def query_back_body(folds, dq_ref, cos_ref, sin_ref, w_ref, *refs):
    old = refs[: 2 * folds]
    turned, gn_ref = refs[2 * folds : 2 * folds + 2]
    fold(old, refs[2 * folds + 2 :])
    cosine, sine = cos_ref[...], sin_ref[...]
    mid = HEAD_DIM // 2
    for head in range(QUERY_HEADS):
        a = dq_ref[HEAD_DIM * head : HEAD_DIM * head + mid, :]
        b = dq_ref[HEAD_DIM * head + mid : HEAD_DIM * head + HEAD_DIM, :]
        turned[HEAD_DIM * head : HEAD_DIM * head + mid, :] = a * cosine + b * sine
        turned[HEAD_DIM * head + mid : HEAD_DIM * head + HEAD_DIM, :] = b * cosine - a * sine
    width = turned.shape[0]
    grad_query = turned[...].T.astype(BF)
    kv_width = 2 * KEY_VALUE_HEADS * HEAD_DIM
    gn_ref[...] = mm_t(grad_query, w_ref[:, kv_width : kv_width + width])


def kv_back_body(custom, groups, turn, idx_ref, *refs):
    dkv_ref, turned, cos_ref, sin_ref, w_ref, n_ref, gn_ref, x_ref, gmid_ref, g_ref = refs[:10]
    refs = refs[10:]
    count = 2 if custom else 1
    c_refs = refs[:count]
    grad_ref, gain_ref, kv_flip, flat, deep_flip = refs[count:]
    parts = 8 if custom else 1
    depths = groups if custom else 1
    dkv = dkv_ref[...]
    cosine, sine = cos_ref[...], -sin_ref[...]
    low = lax.broadcasted_iota(jnp.int32, cosine.shape, 1) < HEAD_DIM
    first = rotate(dkv[:, :128], cosine, sine)
    second = jnp.where(low, rotate(dkv[:, 128:256], cosine, sine), dkv[:, 128:256])
    grad_kv = jnp.concatenate([first, second, dkv[:, 256:]], axis=1)
    kv_flip[...] = grad_kv.T
    normed = n_ref[...]
    kv_width, width = KEY_VALUE_HEADS * HEAD_DIM, turned.shape[0]
    cut = width // depths
    grad_normed = gn_ref[...] + mm_t(grad_kv.astype(BF), w_ref[:, : 2 * kv_width])
    back, gain_grad = norm_back(x_ref[...], g_ref[...], grad_normed)
    grad = gmid_ref[...] + back
    grad_ref[...] = (grad.T if turn else grad).astype(grad_ref.dtype)
    gain_ref[...] = gain_grad
    flat[...] = flip(normed)
    for t, at in enumerate(by_depth(custom, idx_ref, depths, cut)):
        deep_flip[t * cut : t * cut + cut, :] = flat[at, :].astype(BF)
    rows = kv_width // parts
    for half, slot, xor in slots(custom, True):
        if xor is None:
            right = jnp.concatenate([turned[...], kv_flip[...]], axis=0)
        else:
            start = pl.multiple_of((idx_ref[0] ^ xor) * rows, 8)
            right = jnp.concatenate(
                [
                    turned[rows_of(idx_ref, xor, width // parts), :],
                    kv_flip[pl.ds(start, rows), :],
                    kv_flip[pl.ds(kv_width + start, rows), :],
                ],
                axis=0,
            )
        block = mm_t(deep_flip[...], right.astype(BF)).astype(BF)
        for t in range(depths):
            c_refs[half][slot * depths + t] = block[t * cut : t * cut + cut]


def finish_body(*refs):
    parts, gain_ref, came_ref = refs[:12], refs[12], refs[13]
    gq_ref, gk_ref, gv_ref, go_ref, gg_ref, gu_ref, gd_ref, total_ref = refs[14:]
    total_ref[...] = gain_ref[...] + came_ref[...]
    for layer in range(LAYERS):
        total = [
            parts[6 * layer + 2 * i][0].astype(F32) + parts[6 * layer + 2 * i + 1][0].astype(F32)
            for i in range(3)
        ]
        gate_width, rows = gg_ref.shape[2], gd_ref.shape[2]
        gg_ref[layer] = total[0][:, :gate_width]
        gu_ref[layer] = total[0][:, gate_width:]
        gd_ref[layer] = total[1][:, :rows]
        go_ref[layer] = total[1][:, rows:].T
        q_width, k_width = gq_ref.shape[2], gk_ref.shape[2]
        gq_ref[layer] = total[2][:, :q_width]
        gk_ref[layer] = total[2][:, q_width : q_width + k_width]
        gv_ref[layer] = total[2][:, q_width + k_width :]


def attention_unit(layer, wk_ref, wv_ref, wq_ref, wo_ref):
    return jnp.concatenate(
        [wk_ref[layer], wv_ref[layer], wq_ref[layer], wo_ref[layer]], axis=1
    )


def columns_of(idx_ref, width):
    return pl.ds(pl.multiple_of((idx_ref[0] >> 1) * width, 128), width)


def first_pieces_body(idx_ref, wk_ref, wv_ref, wq_ref, wo_ref, unit_ref, piece_ref):
    unit_ref[...] = attention_unit(0, wk_ref, wv_ref, wq_ref, wo_ref)
    rows, cols = piece_ref.shape
    start = pl.multiple_of((idx_ref[0] & 1) * (unit_ref.shape[0] - rows), 16)
    piece_ref[...] = unit_ref[pl.ds(start, rows), columns_of(idx_ref, cols)]


def stack_into(refs, out_ref):
    for i, ref in enumerate(refs):
        out_ref[i] = ref[...]


def put_gate_piece(idx_ref, layer, wg_ref, wu_ref, out_ref):
    rows = wg_ref.shape[1]
    at = columns_of(idx_ref, out_ref.shape[1])

    @pl.when((idx_ref[0] & 1) == 0)
    def _():
        out_ref[:rows, :] = wg_ref[layer, :, at]

    @pl.when((idx_ref[0] & 1) == 1)
    def _():
        out_ref[:rows, :] = wu_ref[layer, :, at]


def put_down_piece(idx_ref, layer, wd_ref, out_ref, base):
    cols = out_ref.shape[1]
    own = wd_ref.shape[1] // 8
    down = wd_ref[layer, pl.ds(pl.multiple_of(idx_ref[0] * own, 16), own), :].astype(F32)
    rest = down[:, cols:]
    out_ref[base : base + own, :] = down[:, :cols].astype(BF)
    out_ref[base + own :, :] = jnp.concatenate(
        [rest[: own // 2], rest[own // 2 :]], axis=1
    ).astype(BF)


def ffn_piece_body(count, idx_ref, *refs):
    column_out, piece_ref = refs[-2:]
    stack_into(refs[:count], column_out)
    wg_ref, wu_ref, wd_ref = refs[count : count + 3]
    put_gate_piece(idx_ref, 0, wg_ref, wu_ref, piece_ref)
    put_down_piece(idx_ref, 0, wd_ref, piece_ref, wg_ref.shape[1])


def second_pieces_body(count, idx_ref, *refs):
    column_out, unit_ref, attention_ref, gate_ref = refs[-4:]
    stack_into(refs[:count], column_out)
    wk_ref, wv_ref, wq_ref, wo_ref, wg_ref, wu_ref, wd_ref = refs[count : count + 7]
    unit_ref[...] = attention_unit(1, wk_ref, wv_ref, wq_ref, wo_ref)
    height = wg_ref.shape[1] - 64
    start = pl.multiple_of((idx_ref[0] & 1) * 64, 16)
    attention_ref[:height, :] = unit_ref[
        pl.ds(start, height), columns_of(idx_ref, attention_ref.shape[1])
    ]
    put_down_piece(idx_ref, 1, wd_ref, attention_ref, height)
    put_gate_piece(idx_ref, 1, wg_ref, wu_ref, gate_ref)


def stack_body(count, *refs):
    stack_into(refs[:count], refs[-1])


def place_all(refs, idx_ref, x_first, group_size, put):
    for combo, ref in enumerate(refs):
        s_bit, c_bit = combo & 1, combo >> 1
        core = (idx_ref[0] & 1) ^ c_bit
        for f_bit in range(2):
            chip = (idx_ref[0] >> 1) ^ ((f_bit + 2 * s_bit) if x_first else (2 * f_bit + s_bit))
            for k in range(group_size - 1):
                depth = lax.rem(idx_ref[1] - (k + 1) + group_size, group_size)
                put(chip, depth, core, ref, f_bit, k)


def put_attention(buf, rows, cols, chip, depth, core, piece):
    at = pl.multiple_of(depth * rows + core * (rows - piece.shape[0]), 16)
    buf[pl.ds(at, piece.shape[0]), pl.ds(pl.multiple_of(chip * (cols // 4), 128), cols // 4)] = piece


def finish_attention(buf, idx_ref, unit_ref, kvq_ref, o_ref):
    rows, cols = unit_ref.shape
    buf[pl.ds(pl.multiple_of(idx_ref[1] * rows, 16), rows), :] = unit_ref[...]
    used = cols - o_ref.shape[1]
    kvq_ref[:, used // 128 * 128 :] = jnp.zeros_like(kvq_ref[:, used // 128 * 128 :])
    kvq_ref[:, :used] = buf[:, :used]
    o_ref[...] = buf[:, used:]


def put_gate(gu_ref, rows, chip, depth, core, piece):
    gu_ref[
        core,
        pl.ds(pl.multiple_of(depth * rows, 16), rows),
        pl.ds(pl.multiple_of(chip * piece.shape[1], 128), piece.shape[1]),
    ] = piece


def put_down(down_ref, rows, chip, depth, core, piece):
    own = rows // 8
    cols = piece.shape[1]
    at = pl.multiple_of(depth * rows + (2 * chip + core) * own, 16)
    down_ref[pl.ds(at, own), :cols] = piece[:own]
    rest = piece[own:].astype(F32)
    wide = down_ref.shape[1] - cols
    down_ref[pl.ds(at, own), cols:] = jnp.concatenate(
        [rest[:, :wide], rest[:, wide:]], axis=0
    ).astype(BF)


def finish_gate(layer, idx_ref, wg_ref, wu_ref, gu_ref):
    rows = wg_ref.shape[1]
    own = pl.ds(pl.multiple_of(idx_ref[1] * rows, 16), rows)
    gu_ref[0, own, :] = wg_ref[layer]
    gu_ref[1, own, :] = wu_ref[layer]


def finish_down(layer, idx_ref, wd_ref, down_ref):
    rows = wd_ref.shape[1]
    down_ref[pl.ds(pl.multiple_of(idx_ref[1] * rows, 16), rows), :] = wd_ref[layer]


def place_first_body(x_first, groups, idx_ref, unit_ref, *refs):
    kvq_ref, o_ref, buf = refs[4:]
    rows, cols = unit_ref.shape

    def put(chip, depth, core, ref, f_bit, k):
        put_attention(buf, rows, cols, chip, depth, core, ref[f_bit, k])

    place_all(refs[:4], idx_ref, x_first, groups, put)
    finish_attention(buf, idx_ref, unit_ref, kvq_ref, o_ref)


def place_ffn_body(x_first, groups, idx_ref, wg_ref, wu_ref, wd_ref, *refs):
    gu_ref, down_ref = refs[4:]
    rows = wg_ref.shape[1]

    def put(chip, depth, core, ref, f_bit, k):
        put_gate(gu_ref, rows, chip, depth, core, ref[f_bit, k, :rows, :])
        put_down(down_ref, wd_ref.shape[1], chip, depth, core, ref[f_bit, k, rows:, :])

    place_all(refs[:4], idx_ref, x_first, groups, put)
    finish_gate(0, idx_ref, wg_ref, wu_ref, gu_ref)
    finish_down(0, idx_ref, wd_ref, down_ref)


def place_second_body(x_first, groups, idx_ref, unit_ref, wd_ref, *refs):
    kvq_ref, o_ref, down_ref, buf = refs[4:]
    rows, cols = unit_ref.shape
    height = rows - 64

    def put(chip, depth, core, ref, f_bit, k):
        put_attention(buf, rows, cols, chip, depth, core, ref[f_bit, k, :height, :])
        put_down(down_ref, wd_ref.shape[1], chip, depth, core, ref[f_bit, k, height:, :])

    place_all(refs[:4], idx_ref, x_first, groups, put)
    finish_attention(buf, idx_ref, unit_ref, kvq_ref, o_ref)
    finish_down(1, idx_ref, wd_ref, down_ref)


def place_gate_body(x_first, groups, idx_ref, wg_ref, wu_ref, *refs):
    gu_ref = refs[4]
    rows = wg_ref.shape[1]

    def put(chip, depth, core, ref, f_bit, k):
        put_gate(gu_ref, rows, chip, depth, core, ref[f_bit, k])

    place_all(refs[:4], idx_ref, x_first, groups, put)
    finish_gate(1, idx_ref, wg_ref, wu_ref, gu_ref)


def xor_pairs(count, bits):
    return [(i, i ^ bits) for i in range(count)]


def swap(value, bits):
    return lax.ppermute(value, "replica", xor_pairs(lax.axis_size("replica"), bits))


def swap_deep(value, bits):
    return lax.ppermute(value, "group", xor_pairs(lax.axis_size("group"), bits))


def from_column(piece):
    groups = lax.axis_size("group")
    return [
        lax.ppermute(piece, "group", [(i, (i + k) % groups) for i in range(groups)])
        for k in range(1, groups)
    ]


def stacked_after(parts, after, name):
    return call(
        functools.partial(stack_body, len(parts)),
        sds((len(parts),) + parts[0].shape),
        [],
        parts,
        after=after,
        limit=4,
        moved=1000000,
        name=name,
    )


def to_all(pair, bits):
    other = swap(pair, bits)
    return pair, other, swap(pair, 1), swap(other, 1)


def gather(value):
    return lax.all_gather(value, "group", axis=0, tiled=True)


def plain_weights(layer, wq, wk, wv, wo, wg, wu, wd):
    pad = jnp.zeros((wq.shape[1], 64), BF)
    return (
        gather(jnp.concatenate([wk[layer], wv[layer], wq[layer], pad], axis=1)),
        gather(wo[layer]),
        jnp.stack([gather(wg[layer]), gather(wu[layer])]),
        gather(wd[layer]),
    )


class Weights:
    def __init__(self, idx, wq, wk, wv, wo, wg, wu, wd):
        self.idx, self.four, self.ffn = idx, [wk, wv, wq, wo], [wg, wu, wd]
        self.groups = lax.axis_size("group")
        self.rows, self.ff = wg.shape[1:]
        self.cols, self.width = self.ff // 4, wo.shape[2]
        self.down_rows = wd.shape[1]
        self.down = wd.shape[1] // 8 * self.width // self.cols
        count = self.groups - 1
        unit, piece = call(
            first_pieces_body,
            [sds((self.rows, self.ff)), sds((self.rows - 64, self.cols))],
            [idx],
            self.four,
            limit=8,
            moved=1000000,
            name="first_pieces",
        )
        column, ffn_piece = call(
            functools.partial(ffn_piece_body, count),
            [sds((count, self.rows - 64, self.cols)), sds((self.rows + self.down, self.cols))],
            [idx],
            [*from_column(piece), *self.ffn],
            limit=8,
            moved=2000000,
            name="ffn_piece",
        )
        self.ffn_column = from_column(ffn_piece)
        pair = stacked_after([column, swap(column, 2)], [], "first_pair")
        arrived = to_all(pair, 4)
        self.first = call(
            functools.partial(place_first_body, True, self.groups),
            self.attention_shapes(),
            [idx],
            [unit, *arrived],
            [pltpu.VMEM((self.rows * self.groups, self.ff), BF)],
            limit=12,
            moved=4000000,
            name="place_first",
        )
        height = self.rows - 64 + self.down
        column, self.unit, attention_piece, gate_piece = call(
            functools.partial(second_pieces_body, count),
            [
                sds((count, self.rows + self.down, self.cols)),
                sds((self.rows, self.ff)),
                sds((height, self.cols)),
                sds((self.rows, self.cols)),
            ],
            [idx],
            [*self.ffn_column, *self.four, *self.ffn],
            after=[arrived[1]],
            limit=8,
            moved=4000000,
            name="second_pieces",
        )
        self.ffn_parts = [column, swap(column, 4)]
        self.second_column = from_column(attention_piece)
        self.gate_piece = gate_piece

    def attention_shapes(self):
        full = self.rows * self.groups
        return [sds((full, 1024)), sds((full, self.width))]

    def gate_shape(self):
        return sds((2, self.rows * self.groups, self.ff))

    def down_shape(self):
        return sds((self.down_rows * self.groups, self.width))

    def after_project(self, token):
        pair = stacked_after(self.ffn_parts, [token], "ffn_pair")
        column = stacked_after(self.second_column, [pair], "second_column")
        self.gate_column = from_column(self.gate_piece)
        self.ffn_arrived = to_all(pair, 2)
        self.second_parts = [column, swap(column, 2)]

    def after_attend(self, token):
        pair = stacked_after(self.second_parts, [token], "second_pair")
        self.second_arrived = to_all(pair, 4)
        column = stacked_after(self.gate_column, [pair], "gate_column")
        self.gate_parts = [column, swap(column, 4)]

    def feed_forward(self):
        return call(
            functools.partial(place_ffn_body, False, self.groups),
            [self.gate_shape(), self.down_shape()],
            [self.idx],
            [*self.ffn, *self.ffn_arrived],
            limit=8,
            moved=10000000,
            name="place_ffn",
        )

    def after_feed_forward(self, token):
        pair = stacked_after(self.gate_parts, [token], "gate_pair")
        self.gate_arrived = to_all(pair, 2)

    def second(self):
        return call(
            functools.partial(place_second_body, True, self.groups),
            self.attention_shapes() + [self.down_shape()],
            [self.idx],
            [self.unit, self.ffn[2], *self.second_arrived],
            [pltpu.VMEM((self.rows * self.groups, self.ff), BF)],
            limit=8,
            moved=8000000,
            name="place_second",
        )

    def gate(self):
        return call(
            functools.partial(place_gate_body, False, self.groups),
            self.gate_shape(),
            [self.idx],
            [*self.ffn[:2], *self.gate_arrived],
            limit=8,
            moved=7000000,
            name="place_gate",
        )


def plus(a, b):
    return (a.astype(F32) + b.astype(F32)).astype(BF)


class Travelling:
    def __init__(self, keep, send, x_first):
        first, second = (2, 4) if x_first else (4, 2)
        self.steps = [(swap, 1), (swap, first), (swap, second), (swap_deep, 1), (swap_deep, 2)]
        self.keep, self.send = keep, send
        self.go()

    def go(self):
        way, bits = self.steps.pop(0)
        self.got = way(self.send, bits)

    def folded(self, low, high):
        self.keep, self.send = low, high
        self.go()


class Gains:
    def __init__(self, value):
        self.steps = [(swap, 1), (swap, 2), (swap, 4), (swap_deep, 1), (swap_deep, 2)]
        self.go(value)

    def go(self, value):
        way, bits = self.steps.pop(0)
        self.value, self.got = value, way(value, bits)


def step(travellers, gains=None, name=None):
    args, outs = fold_with(travellers)
    if gains is not None:
        args = args + [gains.value, gains.got]
        outs = outs + [sds(gains.value.shape, F32)]
    results = call(
        functools.partial(step_body, len(travellers), gains is not None),
        outs,
        [],
        args,
        limit=8,
        moved=2000000,
        name=name,
    )
    fold_done(travellers, results)
    if gains is not None:
        gains.go(results[-1])


def fold_with(travellers):
    args, outs = [], []
    for t in travellers:
        shape = (t.keep.shape[0] // 2,) + t.keep.shape[1:]
        args += [t.keep, t.got]
        outs += [sds(shape), sds(shape)]
    return args, outs


def fold_done(travellers, results):
    for i, t in enumerate(travellers):
        t.folded(results[2 * i], results[2 * i + 1])


def scatter_plain(value):
    part = lax.psum_scatter(value, "replica", scatter_dimension=1, tiled=True)
    return lax.psum_scatter(part, "group", scatter_dimension=0, tiled=True).astype(F32)


def local(
    tokens,
    segments,
    positions,
    cotangent,
    w_query,
    key_weight,
    value_weight,
    w_out,
    w_gate,
    w_up,
    w_down,
    norm_gains,
):
    sequences, length, width = tokens.shape
    replicas, groups = lax.axis_size("replica"), lax.axis_size("group")
    r, z = lax.axis_index("replica"), lax.axis_index("group")
    custom = replicas == 8 and groups == 4
    idx = jnp.stack([r, z]).astype(jnp.int32)
    hidden_width = w_gate.shape[2]
    kv_width = key_weight.shape[2]
    full = length * groups
    core_pairs = xor_pairs(replicas, 1)
    z_pairs = xor_pairs(groups, 1)

    half_way = groups // 2
    exchange = []
    for i in range(replicas):
        for j in range(groups):
            if i % 2 == 1 and j < half_way:
                target = (i - 1, j + half_way)
            elif i % 2 == 0 and j >= half_way:
                target = (i + 1, j - half_way)
            else:
                target = (i, j)
            exchange.append((i * groups + j, target[0] * groups + target[1]))

    def relocate(value):
        return lax.ppermute(value, BOTH, exchange) if custom else value

    def share(value):
        if not custom:
            every = lax.all_gather(value, "group", axis=0, tiled=False)
            return [every[i] for i in range(groups)]
        deep = lax.ppermute(value, "group", z_pairs)
        return [
            value,
            deep,
            lax.ppermute(value, "replica", core_pairs),
            lax.ppermute(deep, "replica", core_pairs),
        ]

    tokens = relocate(tokens.reshape(length, width))
    labels = relocate(jnp.stack([segments.reshape(length), positions.reshape(length)]))
    cotangent = relocate(cotangent.reshape(length, width))
    seg, pos = labels[0], labels[1]
    seg_all = jnp.concatenate(share(seg))
    if custom:
        block_at = lambda c, zz: c * half_way + zz % half_way
        c = r & 1
        blocks = [
            block_at(c, z),
            block_at(c, z ^ 1),
            block_at(c ^ 1, z),
            block_at(c ^ 1, z ^ 1),
        ]
    else:
        blocks = list(range(groups))
    mine_block = blocks[0] if custom else z
    ramp = jnp.arange(length, dtype=jnp.int32)
    place_all_keys = jnp.concatenate([b * length + ramp for b in blocks])
    place = mine_block * length + ramp
    allowed = (seg_all[:, None] == seg[None, :]) & (place_all_keys[:, None] <= place[None, :])
    bias = jnp.where(allowed, 0.0, MASKED).astype(F32)

    half_head = HEAD_DIM // 2
    inverse_freq = jnp.power(
        10000.0, -jnp.arange(half_head, dtype=F32) * (2.0 / HEAD_DIM)
    )
    angles = pos.astype(F32)[:, None] * inverse_freq
    cosine, sine = jnp.cos(angles), jnp.sin(angles)
    cos_wide = jnp.concatenate([cosine] * 4, axis=1)
    sin_wide = jnp.concatenate([-sine, sine] * 2, axis=1)
    cos_flip, sin_flip = cosine.T, sine.T

    matrices = (w_query, key_weight, value_weight, w_out, w_gate, w_up, w_down)
    if custom:
        moving = Weights(idx, *matrices)
        weights = [None] * LAYERS
    else:
        weights = [plain_weights(layer, *matrices) for layer in range(LAYERS)]

    tok_f32 = sds((length, width), F32)
    stream = tokens.astype(F32)
    kept = []
    att_flops = 4 * QUERY_HEADS * HEAD_DIM * length * full
    ffn_flops = 6 * length * width * hidden_width
    for layer in range(LAYERS):
        gains = norm_gains[layer]
        if not custom:
            kvq, wo, gu, down = weights[layer]
        elif layer == 0:
            kvq, wo = moving.first
        else:
            kvq, wo, down = moving.second()
        normed, q, kv = call(
            qkv_body,
            [sds((length, width)), sds((length, 640)), sds((length, 2 * kv_width))],
            [],
            [stream, gains[0:1], kvq, cos_wide, sin_wide],
            flops=2 * length * width * 1024,
            moved=2000000,
            limit=12,
            name="project",
        )
        pieces = share(kv)
        if custom and layer == 0:
            moving.after_project(q)
        attended, lse, middle = call(
            functools.partial(attend_body, groups),
            [sds((length, width)), sds((16, length), F32), tok_f32],
            [],
            [q, *pieces, bias, stream, wo],
            [
                pltpu.VMEM((full, kv_width), BF),
                pltpu.VMEM((kv_width, full), BF),
                pltpu.VMEM((640, length), BF),
                pltpu.VMEM((width, length), F32),
            ],
            flops=4 * att_flops,
            moved=4000000,
            limit=16,
            name="attend",
        )
        if custom and layer == 0:
            moving.after_attend(middle)
            gu, down = moving.feed_forward()
        elif custom:
            gu = moving.gate()
        weights[layer] = (kvq, wo, gu, down)
        kept.append((stream, normed, q, pieces, lse, attended, middle))
        if layer + 1 < LAYERS:
            stream = call(
                ffn_body,
                tok_f32,
                [],
                [middle, gains[1:2], gu, down],
                flops=ffn_flops,
                moved=7000000,
                limit=16,
                name="feed_forward",
            )
            if custom:
                moving.after_feed_forward(stream)

    grad = cotangent
    parts = 8 if custom else 1
    count = 2 if custom else 1
    depths = groups if custom else 1
    blocks_here = parts // count * depths
    gain_rows = [None] * LAYERS
    gate_sums, down_sums, query_sums = [None] * LAYERS, [None] * LAYERS, [None] * LAYERS
    for layer in reversed(range(LAYERS)):
        kvq, wo, gu, down = weights[layer]
        entry, normed, q, pieces, lse, attended, middle = kept[layer]
        gains = norm_gains[layer]

        def blocks_of(rows, cols):
            return [sds((blocks_here, rows, cols))] * count

        last = layer + 1 == LAYERS
        outs = call(
            functools.partial(ffn_back_body, custom, groups, last),
            blocks_of(width // depths, 2 * hidden_width // parts)
            + blocks_of(width // parts, (hidden_width + width) // depths)
            + [tok_f32, sds((length, width)), sds((1, width), F32)]
            + [sds((length, width))] * last,
            [idx],
            [middle, grad, gains[1:2], gu, down, wo, attended],
            [
                pltpu.VMEM((width, length), F32),
                pltpu.VMEM((hidden_width, length), BF),
                pltpu.VMEM((hidden_width, length), BF),
                pltpu.VMEM((width, length), F32),
                pltpu.VMEM((width, length), BF),
                pltpu.VMEM((length, hidden_width), BF),
                pltpu.VMEM((length, hidden_width), BF),
            ],
            flops=3 * ffn_flops,
            moved=16000000,
            limit=24,
            name="feed_forward_back",
        )
        a_parts, b_parts = outs[:count], outs[count : 2 * count]
        grad_mid, grad_att, gain_mid = outs[2 * count : 2 * count + 3]
        if last:
            result = relocate(outs[2 * count + 3])
        if custom:
            gate_sums[layer] = Travelling(*a_parts, True)
            down_sums[layer] = Travelling(*b_parts, False)
        halves = 2 if custom else 1
        above = [gate_sums[1], down_sums[1]] if custom and layer == 0 else []
        fold_args, fold_outs = fold_with(above)
        outs = call(
            functools.partial(attend_back_body, groups, halves, len(above)),
            [sds((width, length), F32)]
            + [sds((full // halves, 2 * kv_width))] * halves
            + fold_outs,
            [],
            [q, *pieces, bias, lse, attended, grad_att, *fold_args],
            [
                pltpu.VMEM((full, 2 * kv_width), BF),
                pltpu.VMEM((kv_width, full), BF),
                pltpu.VMEM((640, length), BF),
                pltpu.VMEM((width, length), BF),
                pltpu.VMEM((width, length), F32),
                pltpu.VMEM((full, kv_width), F32),
                pltpu.VMEM((full, kv_width), F32),
            ],
            flops=10 * att_flops,
            moved=6000000,
            limit=20,
            name="attend_back",
        )
        dq_flip, dkv = outs[0], outs[1 : 1 + halves]
        fold_done(above, outs[1 + halves :])
        if custom:
            got = swap(dkv[1], 1)
            deep = plus(dkv[0][length:], got[length:])
            near = dkv[0][:length].astype(F32) + got[:length].astype(F32)
            dkv_sum = near + swap_deep(deep, 1).astype(F32)
        else:
            dkv_sum = lax.psum_scatter(dkv[0], "group", scatter_dimension=0, tiled=True).astype(F32)
        going = [gate_sums[layer], down_sums[layer], query_sums[1]] if custom else []
        going = [t for t in going if t is not None]
        fold_args, fold_outs = fold_with(going)
        outs = call(
            functools.partial(query_back_body, len(going)),
            [sds((width, length), F32), tok_f32] + fold_outs,
            [],
            [dq_flip, cos_flip, sin_flip, kvq, *fold_args],
            flops=2 * length * width * width,
            moved=6000000,
            limit=8,
            name="query_back",
        )
        turned, grad_normed = outs[:2]
        fold_done(going, outs[2:])
        turn = custom and layer == 0
        outs = call(
            functools.partial(kv_back_body, custom, groups, turn),
            blocks_of(width // depths, (width + 2 * kv_width) // parts)
            + [sds((width, length)) if turn else tok_f32, sds((1, width), F32)],
            [idx],
            [
                dkv_sum,
                turned,
                cos_wide,
                sin_wide,
                kvq,
                normed,
                grad_normed,
                entry,
                grad_mid,
                gains[0:1],
            ],
            [
                pltpu.VMEM((2 * kv_width, length), F32),
                pltpu.VMEM((width, length), F32),
                pltpu.VMEM((width, length), BF),
            ],
            flops=4 * length * width * (width + 2 * kv_width),
            moved=5000000,
            limit=10,
            name="key_value_back",
        )
        c_parts, grad, gain_in = outs[:count], outs[count], outs[count + 1]
        if custom:
            query_sums[layer] = Travelling(*c_parts, True)
        else:
            gate_sums[layer], down_sums[layer] = None, None
            plain = [a_parts[0][0], b_parts[0][0], c_parts[0][0]]
            gate_all, down_all, query_all = plain
            kept[layer] = tuple(
                scatter_plain(v)
                for v in (
                    query_all[:, :width],
                    query_all[:, width : width + kv_width],
                    query_all[:, width + kv_width :],
                    down_all[:, hidden_width:].T,
                    gate_all[:, :hidden_width],
                    gate_all[:, hidden_width:],
                    down_all[:, :hidden_width].T,
                )
            )
        gain_rows[layer] = jnp.concatenate([gain_in, gain_mid])
    gains_here = jnp.concatenate(gain_rows)
    if custom:
        gains = Gains(gains_here)
        gate, down, query = gate_sums, down_sums, query_sums
        step([gate[1], down[1], query[0]], gains, name="sums_one")
        step([gate[0], down[0], query[1]], name="sums_two")
        step([gate[0], down[0], *query, gate[1], down[1]], gains, name="sums_three")
        step([gate[0], down[0], *query], gains, name="sums_four")
        step([query[0]], gains, name="sums_five")
        last = []
        for layer in range(LAYERS):
            for t in (gate[layer], down[layer], query[layer]):
                last += [t.keep, t.got]
        wide = w_query.shape[1]
        *stacked, turned, gain_total = call(
            finish_body,
            [
                sds((LAYERS, wide, width // 8), F32),
                sds((LAYERS, wide, kv_width // 8), F32),
                sds((LAYERS, wide, kv_width // 8), F32),
                sds((LAYERS, wide, width // 8), F32),
                sds((LAYERS, wide, hidden_width // 8), F32),
                sds((LAYERS, wide, hidden_width // 8), F32),
                sds((LAYERS, width // 8, hidden_width // groups), F32),
                sds((2 * LAYERS, width), F32),
            ],
            [],
            last + [gains.value, gains.got],
            limit=8,
            moved=1000000,
            name="finish",
        )
        stacked.append(jnp.swapaxes(turned, 1, 2))
        grad_tokens = relocate(grad).astype(F32).T
    else:
        stacked = [jnp.stack([kept[layer][i] for layer in range(LAYERS)]) for i in range(7)]
        gain_total = lax.psum(gains_here, BOTH)
        grad_tokens = grad
    return (
        result.reshape(sequences, length, width),
        grad_tokens.reshape(sequences, length, width),
        *stacked,
        gain_total.reshape(LAYERS, 2, width),
    )


def solution(mesh):
    sequence = P("replica", "group", None)
    matrix = P(None, "group", None)
    owner = P(None, "group", "replica")
    return jax.shard_map(
        local,
        mesh=mesh,
        in_specs=(sequence, P("replica", "group"), P("replica", "group"), sequence)
        + (matrix,) * 7
        + (P(),),
        out_specs=(sequence, sequence) + (owner,) * 7 + (P(),),
        check_vma=False,
    )
```

```python
import functools

import jax
import jax.numpy as jnp
from jax import lax
from jax.experimental import pallas as pl
from jax.experimental.pallas import tpu as pltpu
from jax.sharding import PartitionSpec as P

QUERY_HEADS = 9
KEY_VALUE_HEADS = 3
HEAD_DIM = 64
LAYERS = 2
EPSILON = 1e-05
MASKED = -1e30
BF = jnp.bfloat16
F32 = jnp.float32
BOTH = ("replica", "group")


def mm(a, b):
    return lax.dot_general(a, b, (((1,), (0,)), ((), ())), preferred_element_type=F32)


def mm_t(a, b):
    return lax.dot_general(a, b, (((1,), (1,)), ((), ())), preferred_element_type=F32)


def flip(value):
    return value.astype(F32).T


def call(
    body, outs, scalars, args, scratch=(), flops=0, moved=0, name=None, after=(), limit=32
):
    vmem = pl.BlockSpec(memory_space=pltpu.VMEM)
    specs = [pl.BlockSpec(memory_space=pltpu.SMEM)] * len(scalars) + [vmem] * len(args)
    specs += [pl.BlockSpec(memory_space=pl.ANY)] * len(after)
    many = isinstance(outs, (list, tuple))
    return pl.pallas_call(
        body,
        out_shape=outs,
        in_specs=specs,
        out_specs=[vmem] * len(outs) if many else vmem,
        scratch_shapes=list(scratch),
        compiler_params=pltpu.CompilerParams(vmem_limit_bytes=limit * 1024 * 1024),
        cost_estimate=pl.CostEstimate(flops=flops, bytes_accessed=moved, transcendentals=0),
        name=name,
    )(*scalars, *args, *after)


def sds(shape, dtype=BF):
    return jax.ShapeDtypeStruct(tuple(shape), dtype)


def rotate(value, cosine, signed_sine):
    lane = lax.broadcasted_iota(jnp.int32, value.shape, 1) % HEAD_DIM
    other = jnp.where(lane < HEAD_DIM // 2, pltpu.roll(value, 96, 1), pltpu.roll(value, 32, 1))
    return value * cosine + other * signed_sine


def qkv_body(x_ref, g_ref, w_ref, cos_ref, sin_ref, n_ref, q_ref, kv_ref):
    x = x_ref[...]
    scale = lax.rsqrt(jnp.mean(x * x, axis=-1, keepdims=True) + EPSILON)
    normed = (x * scale * g_ref[...]).astype(BF)
    n_ref[...] = normed
    raw = mm(normed, w_ref[...])
    cosine, sine = cos_ref[...], sin_ref[...]
    low = lax.broadcasted_iota(jnp.int32, cosine.shape, 1) < HEAD_DIM
    for tile in range(8):
        part = raw[:, 128 * tile : 128 * tile + 128]
        at = slice(128 * tile, 128 * tile + 128)
        if tile == 0:
            kv_ref[:, at] = rotate(part, cosine, sine).astype(BF)
        elif tile == 1:
            kv_ref[:, at] = jnp.where(low, rotate(part, cosine, sine), part).astype(BF)
        elif tile == 2:
            kv_ref[:, at] = part.astype(BF)
        else:
            q_ref[:, 128 * (tile - 3) : 128 * (tile - 2)] = (
                rotate(part, cosine, sine) * 0.125
            ).astype(BF)


def attend_body(pieces, *refs):
    q_ref = refs[0]
    kv_refs = refs[1 : 1 + pieces]
    bias_ref, x_ref, wo_ref, att_ref, lse_ref, mid_ref, k_buf, v_flip, q_flip, att_flip = refs[
        1 + pieces :
    ]
    tokens = q_ref.shape[0]
    half = KEY_VALUE_HEADS * HEAD_DIM
    for p in range(pieces):
        k_buf[p * tokens : (p + 1) * tokens, :] = kv_refs[p][:, :half]
        v_flip[:, p * tokens : (p + 1) * tokens] = flip(kv_refs[p][...])[half:].astype(BF)
    q_flip[...] = flip(q_ref[...]).astype(BF)
    for head in range(QUERY_HEADS):
        group = head // (QUERY_HEADS // KEY_VALUE_HEADS)
        at = slice(HEAD_DIM * head, HEAD_DIM * head + HEAD_DIM)
        kat = slice(HEAD_DIM * group, HEAD_DIM * group + HEAD_DIM)
        scores = mm(k_buf[:, kat], q_flip[at, :]) + bias_ref[...]
        top = jnp.max(scores, axis=0, keepdims=True)
        raised = jnp.exp(scores - top)
        total = jnp.sum(raised, axis=0, keepdims=True)
        out = mm(v_flip[kat, :], raised.astype(BF))
        att_flip[at, :] = out * (1.0 / total)
        lse_ref[head : head + 1, :] = top + jnp.log(total)
    attended = att_flip[...].T.astype(BF)
    att_ref[...] = attended
    mid_ref[...] = x_ref[...] + mm(attended, wo_ref[...])


def ffn_body(mid_ref, g_ref, wgu_ref, wd_ref, out_ref):
    mid = mid_ref[...]
    scale = lax.rsqrt(jnp.mean(mid * mid, axis=-1, keepdims=True) + EPSILON)
    normed = (mid * scale * g_ref[...]).astype(BF)
    gate = mm(normed, wgu_ref[0])
    up = mm(normed, wgu_ref[1])
    hidden = (gate * jax.nn.sigmoid(gate) * up).astype(BF)
    out_ref[...] = (mid + mm(hidden, wd_ref[...])).astype(out_ref.dtype)


def norm_back(value, gain, grad):
    scale = lax.rsqrt(jnp.mean(value * value, axis=-1, keepdims=True) + EPSILON)
    gained = grad * gain
    inner = jnp.mean(gained * value, axis=-1, keepdims=True)
    gain_grad = jnp.sum(grad * value * scale, axis=0, keepdims=True)
    return scale * gained - value * (scale * scale * scale * inner), gain_grad


def slots(custom, x_first):
    if not custom:
        return [(0, 0, None)]
    found = []
    for half in range(2):
        for slot in range(4):
            high, low = slot >> 1, slot & 1
            x_bit, y_bit = (high, low) if x_first else (low, high)
            found.append((half, slot, half + 2 * x_bit + 4 * y_bit))
    return found


def rows_of(idx_ref, xor, rows):
    if xor is None:
        return slice(None)
    return pl.ds(pl.multiple_of((idx_ref[0] ^ xor) * rows, 8), rows)


def by_depth(custom, idx_ref, count, size):
    if not custom:
        return [slice(None)]
    order = [(t & 1) * 2 + (t >> 1) for t in range(count)]
    return [pl.ds(pl.multiple_of((idx_ref[1] ^ t) * size, size & -size), size) for t in order]


def fold(refs, outs):
    for i in range(0, len(refs), 2):
        count = refs[i].shape[0] // 2
        for half in range(2):
            at = slice(half * count, half * count + count)
            total = refs[i][at].astype(F32) + refs[i + 1][at].astype(F32)
            outs[i + half][...] = total.astype(BF)


def step_body(folds, gained, *refs):
    ins = 2 * folds + 2 * gained
    fold(refs[: 2 * folds], refs[ins : ins + 2 * folds])
    if gained:
        refs[-1][...] = refs[2 * folds][...] + refs[2 * folds + 1][...]


def ffn_back_body(custom, groups, last, idx_ref, *refs):
    mid_ref, grad_ref, g_ref, gu_ref, wd_ref, wo_ref, att_ref = refs[:7]
    refs = refs[7:]
    count = 2 if custom else 1
    a_refs, b_refs = refs[:count], refs[count : 2 * count]
    gmid_ref, gatt_ref, gain_ref = refs[2 * count : 2 * count + 3]
    refs = refs[2 * count + 3 :]
    if last:
        result_ref, refs = refs[0], refs[1:]
    branch_flip, gate_flip, up_flip, flat, deep_flip, hidden_buf, hidden_deep = refs
    parts = 8 if custom else 1
    depths = groups if custom else 1
    mid, grad = mid_ref[...], grad_ref[...].astype(F32)
    gain = g_ref[...]
    width, hidden_width = branch_flip.shape[0], gate_flip.shape[0]
    cut, hidden_cut = width // depths, hidden_width // depths
    scale = lax.rsqrt(jnp.mean(mid * mid, axis=-1, keepdims=True) + EPSILON)
    normed = (mid * scale * gain).astype(BF)
    gate = mm(normed, gu_ref[0])
    up = mm(normed, gu_ref[1])
    sig = jax.nn.sigmoid(gate)
    hidden_buf[...] = (gate * sig * up).astype(BF)
    if last:
        result_ref[...] = (mid + mm(hidden_buf[...], wd_ref[...])).astype(BF)
    branch = grad.astype(BF)
    branch_flip[...] = flip(branch)
    grad_hidden = mm_t(branch, wd_ref[...])
    grad_gate = (grad_hidden * up * sig * (1.0 + gate * (1.0 - sig))).astype(BF)
    grad_up = (grad_hidden * gate * sig).astype(BF)
    grad_normed = mm_t(grad_gate, gu_ref[0]) + mm_t(grad_up, gu_ref[1])
    back, gain_grad = norm_back(mid, gain, grad_normed)
    grad_mid = grad + back
    gmid_ref[...] = grad_mid
    gain_ref[...] = gain_grad
    attn = grad_mid.astype(BF)
    gatt_ref[...] = mm_t(attn, wo_ref[...]).astype(BF)
    gate_flip[...] = flip(grad_gate).astype(BF)
    up_flip[...] = flip(grad_up).astype(BF)
    flat[...] = flip(normed)
    for t, at in enumerate(by_depth(custom, idx_ref, depths, cut)):
        deep_flip[t * cut : t * cut + cut, :] = flat[at, :].astype(BF)
    rows = hidden_width // parts
    for half, slot, xor in slots(custom, True):
        at = rows_of(idx_ref, xor, rows)
        right = jnp.concatenate([gate_flip[at, :], up_flip[at, :]], axis=0)
        block = mm_t(deep_flip[...], right).astype(BF)
        for t in range(depths):
            a_refs[half][slot * depths + t] = block[t * cut : t * cut + cut]
    for t, at in enumerate(by_depth(custom, idx_ref, depths, hidden_cut)):
        hidden_deep[:, t * hidden_cut : t * hidden_cut + hidden_cut] = hidden_buf[:, at]
    rows = width // parts
    for half, slot, xor in slots(custom, False):
        left = branch_flip[rows_of(idx_ref, xor, rows), :].astype(BF)
        block = mm(left, hidden_deep[...]).astype(BF)
        for t in range(depths):
            b_refs[half][slot * depths + t, :, :hidden_cut] = block[
                :, t * hidden_cut : t * hidden_cut + hidden_cut
            ]
    flat[...] = flip(att_ref[...])
    for t, at in enumerate(by_depth(custom, idx_ref, depths, cut)):
        deep_flip[t * cut : t * cut + cut, :] = flat[at, :].astype(BF)
    branch_flip[...] = flip(attn)
    for half, slot, xor in slots(custom, False):
        left = branch_flip[rows_of(idx_ref, xor, rows), :].astype(BF)
        block = mm_t(left, deep_flip[...]).astype(BF)
        for t in range(depths):
            b_refs[half][slot * depths + t, :, hidden_cut:] = block[:, t * cut : t * cut + cut]


def attend_back_body(pieces, halves, folds, *refs):
    q_ref = refs[0]
    kv_refs = refs[1 : 1 + pieces]
    bias_ref, lse_ref, att_ref, gatt_ref = refs[1 + pieces : 5 + pieces]
    old = refs[5 + pieces : 5 + pieces + 2 * folds]
    refs = refs[5 + pieces + 2 * folds :]
    dq_ref, dkv_refs = refs[0], refs[1 : 1 + halves]
    fold(old, refs[1 + halves : 1 + halves + 2 * folds])
    kv_buf, k_flip, q_flip, g_flip, att_flip, dk_buf, dv_buf = refs[1 + halves + 2 * folds :]
    tokens = q_ref.shape[0]
    half = KEY_VALUE_HEADS * HEAD_DIM
    for p in range(pieces):
        kv_buf[p * tokens : (p + 1) * tokens, :] = kv_refs[p][...]
        k_flip[:, p * tokens : (p + 1) * tokens] = flip(kv_refs[p][...])[:half].astype(BF)
    q_flip[...] = flip(q_ref[...]).astype(BF)
    g_flip[...] = flip(gatt_ref[...]).astype(BF)
    att_flip[...] = flip(att_ref[...])
    per = QUERY_HEADS // KEY_VALUE_HEADS
    for group in range(KEY_VALUE_HEADS):
        kat = slice(HEAD_DIM * group, HEAD_DIM * group + HEAD_DIM)
        vat = slice(half + HEAD_DIM * group, half + HEAD_DIM * group + HEAD_DIM)
        dk = dv = None
        for head in range(per * group, per * group + per):
            at = slice(HEAD_DIM * head, HEAD_DIM * head + HEAD_DIM)
            scores = mm(kv_buf[:, kat], q_flip[at, :]) + bias_ref[...]
            probs = jnp.exp(scores - lse_ref[head : head + 1, :])
            grad_probs = mm(kv_buf[:, vat], g_flip[at, :])
            row_dot = jnp.sum(
                g_flip[at, :].astype(F32) * att_flip[at, :], axis=0, keepdims=True
            )
            grad_scores = (probs * (grad_probs - row_dot)).astype(BF)
            dv_part = mm(probs.astype(BF), gatt_ref[:, at])
            dk_part = mm(grad_scores, q_ref[:, at])
            dv = dv_part if dv is None else dv + dv_part
            dk = dk_part if dk is None else dk + dk_part
            dq_ref[at, :] = mm(k_flip[kat, :], grad_scores) * 0.125
        dk_buf[:, kat] = dk
        dv_buf[:, kat] = dv
    rows = dk_buf.shape[0] // halves
    for h in range(halves):
        at = slice(h * rows, h * rows + rows)
        dkv_refs[h][:, :half] = dk_buf[at, :].astype(BF)
        dkv_refs[h][:, half:] = dv_buf[at, :].astype(BF)


def query_back_body(folds, dq_ref, cos_ref, sin_ref, w_ref, *refs):
    old = refs[: 2 * folds]
    turned, gn_ref = refs[2 * folds : 2 * folds + 2]
    fold(old, refs[2 * folds + 2 :])
    cosine, sine = cos_ref[...], sin_ref[...]
    mid = HEAD_DIM // 2
    for head in range(QUERY_HEADS):
        a = dq_ref[HEAD_DIM * head : HEAD_DIM * head + mid, :]
        b = dq_ref[HEAD_DIM * head + mid : HEAD_DIM * head + HEAD_DIM, :]
        turned[HEAD_DIM * head : HEAD_DIM * head + mid, :] = a * cosine + b * sine
        turned[HEAD_DIM * head + mid : HEAD_DIM * head + HEAD_DIM, :] = b * cosine - a * sine
    width = turned.shape[0]
    grad_query = turned[...].T.astype(BF)
    kv_width = 2 * KEY_VALUE_HEADS * HEAD_DIM
    gn_ref[...] = mm_t(grad_query, w_ref[:, kv_width : kv_width + width])


def kv_back_body(custom, groups, turn, idx_ref, *refs):
    dkv_ref, turned, cos_ref, sin_ref, w_ref, n_ref, gn_ref, x_ref, gmid_ref, g_ref = refs[:10]
    refs = refs[11:]
    count = 2 if custom else 1
    c_refs = refs[:count]
    grad_ref, gain_ref, kv_flip, flat, deep_flip = refs[count:]
    parts = 8 if custom else 1
    depths = groups if custom else 1
    dkv = dkv_ref[...]
    cosine, sine = cos_ref[...], -sin_ref[...]
    low = lax.broadcasted_iota(jnp.int32, cosine.shape, 1) < HEAD_DIM
    first = rotate(dkv[:, :128], cosine, sine)
    second = jnp.where(low, rotate(dkv[:, 128:256], cosine, sine), dkv[:, 128:256])
    grad_kv = jnp.concatenate([first, second, dkv[:, 256:]], axis=1)
    kv_flip[...] = grad_kv.T
    normed = n_ref[...]
    kv_width, width = KEY_VALUE_HEADS * HEAD_DIM, turned.shape[0]
    cut = width // depths
    grad_normed = gn_ref[...] + mm_t(grad_kv.astype(BF), w_ref[:, : 2 * kv_width])
    back, gain_grad = norm_back(x_ref[...], g_ref[...], grad_normed)
    grad = gmid_ref[...] + back
    grad_ref[...] = (grad.T if turn else grad).astype(grad_ref.dtype)
    gain_ref[...] = gain_grad
    flat[...] = flip(normed)
    for t, at in enumerate(by_depth(custom, idx_ref, depths, cut)):
        deep_flip[t * cut : t * cut + cut, :] = flat[at, :].astype(BF)
    rows = kv_width // parts
    for half, slot, xor in slots(custom, True):
        if xor is None:
            right = jnp.concatenate([turned[...], kv_flip[...]], axis=0)
        else:
            start = pl.multiple_of((idx_ref[0] ^ xor) * rows, 8)
            right = jnp.concatenate(
                [
                    turned[rows_of(idx_ref, xor, width // parts), :],
                    kv_flip[pl.ds(start, rows), :],
                    kv_flip[pl.ds(kv_width + start, rows), :],
                ],
                axis=0,
            )
        block = mm_t(deep_flip[...], right.astype(BF)).astype(BF)
        for t in range(depths):
            c_refs[half][slot * depths + t] = block[t * cut : t * cut + cut]


def finish_body(*refs):
    parts, gain_ref, came_ref = refs[:12], refs[12], refs[13]
    gq_ref, gk_ref, gv_ref, go_ref, gg_ref, gu_ref, gd_ref, total_ref = refs[14:]
    total_ref[...] = gain_ref[...] + came_ref[...]
    for layer in range(LAYERS):
        total = [
            parts[6 * layer + 2 * i][0].astype(F32) + parts[6 * layer + 2 * i + 1][0].astype(F32)
            for i in range(3)
        ]
        gate_width, rows = gg_ref.shape[2], gd_ref.shape[2]
        gg_ref[layer] = total[0][:, :gate_width]
        gu_ref[layer] = total[0][:, gate_width:]
        gd_ref[layer] = total[1][:, :rows]
        go_ref[layer] = total[1][:, rows:].T
        q_width, k_width = gq_ref.shape[2], gk_ref.shape[2]
        gq_ref[layer] = total[2][:, :q_width]
        gk_ref[layer] = total[2][:, q_width : q_width + k_width]
        gv_ref[layer] = total[2][:, q_width + k_width :]


def attention_unit(layer, wk_ref, wv_ref, wq_ref, wo_ref):
    return jnp.concatenate(
        [wk_ref[layer], wv_ref[layer], wq_ref[layer], wo_ref[layer]], axis=1
    )


def columns_of(idx_ref, width):
    return pl.ds(pl.multiple_of((idx_ref[0] >> 1) * width, 128), width)


def first_pieces_body(idx_ref, wk_ref, wv_ref, wq_ref, wo_ref, unit_ref, piece_ref):
    unit_ref[...] = attention_unit(0, wk_ref, wv_ref, wq_ref, wo_ref)
    rows, cols = piece_ref.shape
    start = pl.multiple_of((idx_ref[0] & 1) * (unit_ref.shape[0] - rows), 16)
    piece_ref[...] = unit_ref[pl.ds(start, rows), columns_of(idx_ref, cols)]


def stack_into(refs, out_ref):
    for i, ref in enumerate(refs):
        out_ref[i] = ref[...]


def put_gate_piece(idx_ref, layer, wg_ref, wu_ref, out_ref):
    rows = wg_ref.shape[1]
    at = columns_of(idx_ref, out_ref.shape[1])

    @pl.when((idx_ref[0] & 1) == 0)
    def _():
        out_ref[:rows, :] = wg_ref[layer, :, at]

    @pl.when((idx_ref[0] & 1) == 1)
    def _():
        out_ref[:rows, :] = wu_ref[layer, :, at]


def put_down_piece(idx_ref, layer, wd_ref, out_ref, base):
    cols = out_ref.shape[1]
    own = wd_ref.shape[1] // 8
    down = wd_ref[layer, pl.ds(pl.multiple_of(idx_ref[0] * own, 16), own), :].astype(F32)
    rest = down[:, cols:]
    out_ref[base : base + own, :] = down[:, :cols].astype(BF)
    out_ref[base + own :, :] = jnp.concatenate(
        [rest[: own // 2], rest[own // 2 :]], axis=1
    ).astype(BF)


def ffn_piece_body(count, idx_ref, *refs):
    column_out, piece_ref = refs[-2:]
    stack_into(refs[:count], column_out)
    wg_ref, wu_ref, wd_ref = refs[count : count + 3]
    put_gate_piece(idx_ref, 0, wg_ref, wu_ref, piece_ref)
    put_down_piece(idx_ref, 0, wd_ref, piece_ref, wg_ref.shape[1])


def second_pieces_body(count, idx_ref, *refs):
    column_out, unit_ref, attention_ref, gate_ref = refs[-4:]
    stack_into(refs[:count], column_out)
    wk_ref, wv_ref, wq_ref, wo_ref, wg_ref, wu_ref, wd_ref = refs[count : count + 7]
    unit_ref[...] = attention_unit(1, wk_ref, wv_ref, wq_ref, wo_ref)
    height = wg_ref.shape[1] - 64
    start = pl.multiple_of((idx_ref[0] & 1) * 64, 16)
    attention_ref[:height, :] = unit_ref[
        pl.ds(start, height), columns_of(idx_ref, attention_ref.shape[1])
    ]
    put_down_piece(idx_ref, 1, wd_ref, attention_ref, height)
    put_gate_piece(idx_ref, 1, wg_ref, wu_ref, gate_ref)


def stack_body(count, *refs):
    stack_into(refs[:count], refs[-1])


def place_all(refs, idx_ref, x_first, group_size, put):
    for combo, ref in enumerate(refs):
        s_bit, c_bit = combo & 1, combo >> 1
        core = (idx_ref[0] & 1) ^ c_bit
        for f_bit in range(2):
            chip = (idx_ref[0] >> 1) ^ ((f_bit + 2 * s_bit) if x_first else (2 * f_bit + s_bit))
            for k in range(group_size - 1):
                depth = lax.rem(idx_ref[1] - (k + 1) + group_size, group_size)
                put(chip, depth, core, ref, f_bit, k)


def put_attention(buf, rows, cols, chip, depth, core, piece):
    at = pl.multiple_of(depth * rows + core * (rows - piece.shape[0]), 16)
    buf[pl.ds(at, piece.shape[0]), pl.ds(pl.multiple_of(chip * (cols // 4), 128), cols // 4)] = piece


def finish_attention(buf, idx_ref, unit_ref, kvq_ref, o_ref):
    rows, cols = unit_ref.shape
    buf[pl.ds(pl.multiple_of(idx_ref[1] * rows, 16), rows), :] = unit_ref[...]
    used = cols - o_ref.shape[1]
    kvq_ref[:, used // 128 * 128 :] = jnp.zeros_like(kvq_ref[:, used // 128 * 128 :])
    kvq_ref[:, :used] = buf[:, :used]
    o_ref[...] = buf[:, used:]


def put_gate(gu_ref, rows, chip, depth, core, piece):
    gu_ref[
        core,
        pl.ds(pl.multiple_of(depth * rows, 16), rows),
        pl.ds(pl.multiple_of(chip * piece.shape[1], 128), piece.shape[1]),
    ] = piece


def put_down(down_ref, rows, chip, depth, core, piece):
    own = rows // 8
    cols = piece.shape[1]
    at = pl.multiple_of(depth * rows + (2 * chip + core) * own, 16)
    down_ref[pl.ds(at, own), :cols] = piece[:own]
    rest = piece[own:].astype(F32)
    wide = down_ref.shape[1] - cols
    down_ref[pl.ds(at, own), cols:] = jnp.concatenate(
        [rest[:, :wide], rest[:, wide:]], axis=0
    ).astype(BF)


def finish_gate(layer, idx_ref, wg_ref, wu_ref, gu_ref):
    rows = wg_ref.shape[1]
    own = pl.ds(pl.multiple_of(idx_ref[1] * rows, 16), rows)
    gu_ref[0, own, :] = wg_ref[layer]
    gu_ref[1, own, :] = wu_ref[layer]


def finish_down(layer, idx_ref, wd_ref, down_ref):
    rows = wd_ref.shape[1]
    down_ref[pl.ds(pl.multiple_of(idx_ref[1] * rows, 16), rows), :] = wd_ref[layer]


def place_first_body(x_first, groups, idx_ref, unit_ref, *refs):
    kvq_ref, o_ref, buf = refs[4:]
    rows, cols = unit_ref.shape

    def put(chip, depth, core, ref, f_bit, k):
        put_attention(buf, rows, cols, chip, depth, core, ref[f_bit, k])

    place_all(refs[:4], idx_ref, x_first, groups, put)
    finish_attention(buf, idx_ref, unit_ref, kvq_ref, o_ref)


def place_ffn_body(x_first, groups, idx_ref, wg_ref, wu_ref, wd_ref, *refs):
    gu_ref, down_ref = refs[4:]
    rows = wg_ref.shape[1]

    def put(chip, depth, core, ref, f_bit, k):
        put_gate(gu_ref, rows, chip, depth, core, ref[f_bit, k, :rows, :])
        put_down(down_ref, wd_ref.shape[1], chip, depth, core, ref[f_bit, k, rows:, :])

    place_all(refs[:4], idx_ref, x_first, groups, put)
    finish_gate(0, idx_ref, wg_ref, wu_ref, gu_ref)
    finish_down(0, idx_ref, wd_ref, down_ref)


def place_second_body(x_first, groups, idx_ref, unit_ref, wd_ref, *refs):
    kvq_ref, o_ref, down_ref, buf = refs[4:]
    rows, cols = unit_ref.shape
    height = rows - 64

    def put(chip, depth, core, ref, f_bit, k):
        put_attention(buf, rows, cols, chip, depth, core, ref[f_bit, k, :height, :])
        put_down(down_ref, wd_ref.shape[1], chip, depth, core, ref[f_bit, k, height:, :])

    place_all(refs[:4], idx_ref, x_first, groups, put)
    finish_attention(buf, idx_ref, unit_ref, kvq_ref, o_ref)
    finish_down(1, idx_ref, wd_ref, down_ref)


def place_gate_body(x_first, groups, idx_ref, wg_ref, wu_ref, *refs):
    gu_ref = refs[4]
    rows = wg_ref.shape[1]

    def put(chip, depth, core, ref, f_bit, k):
        put_gate(gu_ref, rows, chip, depth, core, ref[f_bit, k])

    place_all(refs[:4], idx_ref, x_first, groups, put)
    finish_gate(1, idx_ref, wg_ref, wu_ref, gu_ref)


def xor_pairs(count, bits):
    return [(i, i ^ bits) for i in range(count)]


def swap(value, bits):
    return lax.ppermute(value, "replica", xor_pairs(lax.axis_size("replica"), bits))


def swap_deep(value, bits):
    return lax.ppermute(value, "group", xor_pairs(lax.axis_size("group"), bits))


def from_column(piece):
    groups = lax.axis_size("group")
    return [
        lax.ppermute(piece, "group", [(i, (i + k) % groups) for i in range(groups)])
        for k in range(1, groups)
    ]


def stacked_after(parts, after, name):
    return call(
        functools.partial(stack_body, len(parts)),
        sds((len(parts),) + parts[0].shape),
        [],
        parts,
        after=after,
        limit=4,
        moved=1000000,
        name=name,
    )


def to_all(pair, bits):
    other = swap(pair, bits)
    return pair, other, swap(pair, 1), swap(other, 1)


def gather(value):
    return lax.all_gather(value, "group", axis=0, tiled=True)


def plain_weights(layer, wq, wk, wv, wo, wg, wu, wd):
    pad = jnp.zeros((wq.shape[1], 64), BF)
    return (
        gather(jnp.concatenate([wk[layer], wv[layer], wq[layer], pad], axis=1)),
        gather(wo[layer]),
        jnp.stack([gather(wg[layer]), gather(wu[layer])]),
        gather(wd[layer]),
    )


class Weights:
    def __init__(self, idx, wq, wk, wv, wo, wg, wu, wd):
        self.idx, self.four, self.ffn = idx, [wk, wv, wq, wo], [wg, wu, wd]
        self.groups = lax.axis_size("group")
        self.rows, self.ff = wg.shape[1:]
        self.cols, self.width = self.ff // 4, wo.shape[2]
        self.down_rows = wd.shape[1]
        self.down = wd.shape[1] // 8 * self.width // self.cols
        count = self.groups - 1
        unit, piece = call(
            first_pieces_body,
            [sds((self.rows, self.ff)), sds((self.rows - 64, self.cols))],
            [idx],
            self.four,
            limit=8,
            moved=1000000,
            name="first_pieces",
        )
        column, ffn_piece = call(
            functools.partial(ffn_piece_body, count),
            [sds((count, self.rows - 64, self.cols)), sds((self.rows + self.down, self.cols))],
            [idx],
            [*from_column(piece), *self.ffn],
            limit=8,
            moved=2000000,
            name="ffn_piece",
        )
        self.ffn_column = from_column(ffn_piece)
        pair = stacked_after([column, swap(column, 2)], [], "first_pair")
        arrived = to_all(pair, 4)
        self.first = call(
            functools.partial(place_first_body, True, self.groups),
            self.attention_shapes(),
            [idx],
            [unit, *arrived],
            [pltpu.VMEM((self.rows * self.groups, self.ff), BF)],
            limit=12,
            moved=4000000,
            name="place_first",
        )
        height = self.rows - 64 + self.down
        column, self.unit, attention_piece, gate_piece = call(
            functools.partial(second_pieces_body, count),
            [
                sds((count, self.rows + self.down, self.cols)),
                sds((self.rows, self.ff)),
                sds((height, self.cols)),
                sds((self.rows, self.cols)),
            ],
            [idx],
            [*self.ffn_column, *self.four, *self.ffn],
            after=[arrived[1]],
            limit=8,
            moved=4000000,
            name="second_pieces",
        )
        self.ffn_parts = [column, swap(column, 4)]
        self.second_column = from_column(attention_piece)
        self.gate_piece = gate_piece

    def attention_shapes(self):
        full = self.rows * self.groups
        return [sds((full, 1024)), sds((full, self.width))]

    def gate_shape(self):
        return sds((2, self.rows * self.groups, self.ff))

    def down_shape(self):
        return sds((self.down_rows * self.groups, self.width))

    def after_project(self, token):
        pair = stacked_after(self.ffn_parts, [token], "ffn_pair")
        column = stacked_after(self.second_column, [pair], "second_column")
        self.gate_column = from_column(self.gate_piece)
        self.ffn_arrived = to_all(pair, 2)
        self.second_parts = [column, swap(column, 2)]

    def after_attend(self, token):
        pair = stacked_after(self.second_parts, [token], "second_pair")
        self.second_arrived = to_all(pair, 4)
        column = stacked_after(self.gate_column, [pair], "gate_column")
        self.gate_parts = [column, swap(column, 4)]

    def feed_forward(self):
        return call(
            functools.partial(place_ffn_body, False, self.groups),
            [self.gate_shape(), self.down_shape()],
            [self.idx],
            [*self.ffn, *self.ffn_arrived],
            limit=8,
            moved=10000000,
            name="place_ffn",
        )

    def after_feed_forward(self, token):
        pair = stacked_after(self.gate_parts, [token], "gate_pair")
        self.gate_arrived = to_all(pair, 2)

    def second(self):
        return call(
            functools.partial(place_second_body, True, self.groups),
            self.attention_shapes() + [self.down_shape()],
            [self.idx],
            [self.unit, self.ffn[2], *self.second_arrived],
            [pltpu.VMEM((self.rows * self.groups, self.ff), BF)],
            limit=8,
            moved=8000000,
            name="place_second",
        )

    def gate(self):
        return call(
            functools.partial(place_gate_body, False, self.groups),
            self.gate_shape(),
            [self.idx],
            [*self.ffn[:2], *self.gate_arrived],
            limit=8,
            moved=7000000,
            name="place_gate",
        )


def plus(a, b):
    return (a.astype(F32) + b.astype(F32)).astype(BF)


class Travelling:
    def __init__(self, keep, send, x_first):
        first, second = (2, 4) if x_first else (4, 2)
        self.steps = [(swap, 1), (swap, first), (swap, second), (swap_deep, 1), (swap_deep, 2)]
        self.keep, self.send = keep, send
        self.go()

    def go(self):
        way, bits = self.steps.pop(0)
        self.got = way(self.send, bits)

    def folded(self, low, high):
        self.keep, self.send = low, high
        self.go()


class Gains:
    def __init__(self, value):
        self.steps = [(swap, 1), (swap, 2), (swap, 4), (swap_deep, 1), (swap_deep, 2)]
        self.go(value)

    def go(self, value):
        way, bits = self.steps.pop(0)
        self.value, self.got = value, way(value, bits)


def step(travellers, gains=None, name=None):
    args, outs = fold_with(travellers)
    if gains is not None:
        args = args + [gains.value, gains.got]
        outs = outs + [sds(gains.value.shape, F32)]
    results = call(
        functools.partial(step_body, len(travellers), gains is not None),
        outs,
        [],
        args,
        limit=8,
        moved=2000000,
        name=name,
    )
    fold_done(travellers, results)
    if gains is not None:
        gains.go(results[-1])


def fold_with(travellers):
    args, outs = [], []
    for t in travellers:
        shape = (t.keep.shape[0] // 2,) + t.keep.shape[1:]
        args += [t.keep, t.got]
        outs += [sds(shape), sds(shape)]
    return args, outs


def fold_done(travellers, results):
    for i, t in enumerate(travellers):
        t.folded(results[2 * i], results[2 * i + 1])


def scatter_plain(value):
    part = lax.psum_scatter(value, "replica", scatter_dimension=1, tiled=True)
    return lax.psum_scatter(part, "group", scatter_dimension=0, tiled=True).astype(F32)


def local(
    tokens,
    segments,
    positions,
    cotangent,
    w_query,
    key_weight,
    value_weight,
    w_out,
    w_gate,
    w_up,
    w_down,
    norm_gains,
):
    sequences, length, width = tokens.shape
    replicas, groups = lax.axis_size("replica"), lax.axis_size("group")
    r, z = lax.axis_index("replica"), lax.axis_index("group")
    custom = replicas == 8 and groups == 4
    idx = jnp.stack([r, z]).astype(jnp.int32)
    hidden_width = w_gate.shape[2]
    kv_width = key_weight.shape[2]
    full = length * groups
    core_pairs = xor_pairs(replicas, 1)
    z_pairs = xor_pairs(groups, 1)

    half_way = groups // 2
    exchange = []
    for i in range(replicas):
        for j in range(groups):
            if i % 2 == 1 and j < half_way:
                target = (i - 1, j + half_way)
            elif i % 2 == 0 and j >= half_way:
                target = (i + 1, j - half_way)
            else:
                target = (i, j)
            exchange.append((i * groups + j, target[0] * groups + target[1]))

    def relocate(value):
        return lax.ppermute(value, BOTH, exchange) if custom else value

    def share(value):
        if not custom:
            every = lax.all_gather(value, "group", axis=0, tiled=False)
            return [every[i] for i in range(groups)]
        deep = lax.ppermute(value, "group", z_pairs)
        return [
            value,
            deep,
            lax.ppermute(value, "replica", core_pairs),
            lax.ppermute(deep, "replica", core_pairs),
        ]

    tokens = relocate(tokens.reshape(length, width))
    labels = relocate(jnp.stack([segments.reshape(length), positions.reshape(length)]))
    cotangent = relocate(cotangent.reshape(length, width))
    seg, pos = labels[0], labels[1]
    seg_all = jnp.concatenate(share(seg))
    if custom:
        block_at = lambda c, zz: c * half_way + zz % half_way
        c = r & 1
        blocks = [
            block_at(c, z),
            block_at(c, z ^ 1),
            block_at(c ^ 1, z),
            block_at(c ^ 1, z ^ 1),
        ]
    else:
        blocks = list(range(groups))
    mine_block = blocks[0] if custom else z
    ramp = jnp.arange(length, dtype=jnp.int32)
    place_all_keys = jnp.concatenate([b * length + ramp for b in blocks])
    place = mine_block * length + ramp
    allowed = (seg_all[:, None] == seg[None, :]) & (place_all_keys[:, None] <= place[None, :])
    bias = jnp.where(allowed, 0.0, MASKED).astype(F32)

    half_head = HEAD_DIM // 2
    inverse_freq = jnp.power(
        10000.0, -jnp.arange(half_head, dtype=F32) * (2.0 / HEAD_DIM)
    )
    angles = pos.astype(F32)[:, None] * inverse_freq
    cosine, sine = jnp.cos(angles), jnp.sin(angles)
    cos_wide = jnp.concatenate([cosine] * 4, axis=1)
    sin_wide = jnp.concatenate([-sine, sine] * 2, axis=1)
    cos_flip, sin_flip = cosine.T, sine.T

    matrices = (w_query, key_weight, value_weight, w_out, w_gate, w_up, w_down)
    if custom:
        moving = Weights(idx, *matrices)
        weights = [None] * LAYERS
    else:
        weights = [plain_weights(layer, *matrices) for layer in range(LAYERS)]

    tok_f32 = sds((length, width), F32)
    stream = tokens.astype(F32)
    kept = []
    att_flops = 4 * QUERY_HEADS * HEAD_DIM * length * full
    ffn_flops = 6 * length * width * hidden_width
    for layer in range(LAYERS):
        gains = norm_gains[layer]
        if not custom:
            kvq, wo, gu, down = weights[layer]
        elif layer == 0:
            kvq, wo = moving.first
        else:
            kvq, wo, down = moving.second()
        normed, q, kv = call(
            qkv_body,
            [sds((length, width)), sds((length, 640)), sds((length, 2 * kv_width))],
            [],
            [stream, gains[0:1], kvq, cos_wide, sin_wide],
            flops=2 * length * width * 1024,
            moved=2000000,
            limit=12,
            name="project",
        )
        pieces = share(kv)
        if custom and layer == 0:
            moving.after_project(q)
        attended, lse, middle = call(
            functools.partial(attend_body, groups),
            [sds((length, width)), sds((16, length), F32), tok_f32],
            [],
            [q, *pieces, bias, stream, wo],
            [
                pltpu.VMEM((full, kv_width), BF),
                pltpu.VMEM((kv_width, full), BF),
                pltpu.VMEM((640, length), BF),
                pltpu.VMEM((width, length), F32),
            ],
            flops=4 * att_flops,
            moved=4000000,
            limit=16,
            name="attend",
        )
        if custom and layer == 0:
            moving.after_attend(middle)
            gu, down = moving.feed_forward()
        elif custom:
            gu = moving.gate()
        weights[layer] = (kvq, wo, gu, down)
        kept.append((stream, normed, q, pieces, lse, attended, middle))
        if layer + 1 < LAYERS:
            stream = call(
                ffn_body,
                tok_f32,
                [],
                [middle, gains[1:2], gu, down],
                flops=ffn_flops,
                moved=7000000,
                limit=16,
                name="feed_forward",
            )
            if custom:
                moving.after_feed_forward(stream)

    grad = cotangent
    parts = 8 if custom else 1
    count = 2 if custom else 1
    depths = groups if custom else 1
    blocks_here = parts // count * depths
    gain_rows = [None] * LAYERS
    gate_sums, down_sums, query_sums = [None] * LAYERS, [None] * LAYERS, [None] * LAYERS
    for layer in reversed(range(LAYERS)):
        kvq, wo, gu, down = weights[layer]
        entry, normed, q, pieces, lse, attended, middle = kept[layer]
        gains = norm_gains[layer]

        def blocks_of(rows, cols):
            return [sds((blocks_here, rows, cols))] * count

        last = layer + 1 == LAYERS
        outs = call(
            functools.partial(ffn_back_body, custom, groups, last),
            blocks_of(width // depths, 2 * hidden_width // parts)
            + blocks_of(width // parts, (hidden_width + width) // depths)
            + [tok_f32, sds((length, width)), sds((1, width), F32)]
            + [sds((length, width))] * last,
            [idx],
            [middle, grad, gains[1:2], gu, down, wo, attended],
            [
                pltpu.VMEM((width, length), F32),
                pltpu.VMEM((hidden_width, length), BF),
                pltpu.VMEM((hidden_width, length), BF),
                pltpu.VMEM((width, length), F32),
                pltpu.VMEM((width, length), BF),
                pltpu.VMEM((length, hidden_width), BF),
                pltpu.VMEM((length, hidden_width), BF),
            ],
            flops=3 * ffn_flops,
            moved=16000000,
            limit=24,
            name="feed_forward_back",
        )
        a_parts, b_parts = outs[:count], outs[count : 2 * count]
        grad_mid, grad_att, gain_mid = outs[2 * count : 2 * count + 3]
        if last:
            result = relocate(outs[2 * count + 3])
        if custom:
            gate_sums[layer] = Travelling(*a_parts, True)
            down_sums[layer] = Travelling(*b_parts, False)
        halves = 2 if custom else 1
        above = [gate_sums[1], down_sums[1]] if custom and layer == 0 else []
        fold_args, fold_outs = fold_with(above)
        outs = call(
            functools.partial(attend_back_body, groups, halves, len(above)),
            [sds((width, length), F32)]
            + [sds((full // halves, 2 * kv_width))] * halves
            + fold_outs,
            [],
            [q, *pieces, bias, lse, attended, grad_att, *fold_args],
            [
                pltpu.VMEM((full, 2 * kv_width), BF),
                pltpu.VMEM((kv_width, full), BF),
                pltpu.VMEM((640, length), BF),
                pltpu.VMEM((width, length), BF),
                pltpu.VMEM((width, length), F32),
                pltpu.VMEM((full, kv_width), F32),
                pltpu.VMEM((full, kv_width), F32),
            ],
            flops=10 * att_flops,
            moved=6000000,
            limit=20,
            name="attend_back",
        )
        dq_flip, dkv = outs[0], outs[1 : 1 + halves]
        fold_done(above, outs[1 + halves :])
        if custom:
            got = swap(dkv[1], 1)
            deep = plus(dkv[0][length:], got[length:])
            near = dkv[0][:length].astype(F32) + got[:length].astype(F32)
            dkv_sum = near + swap_deep(deep, 1).astype(F32)
        else:
            dkv_sum = lax.psum_scatter(dkv[0], "group", scatter_dimension=0, tiled=True).astype(F32)
        going = [gate_sums[layer], down_sums[layer], query_sums[1]] if custom else []
        going = [t for t in going if t is not None]
        fold_args, fold_outs = fold_with(going)
        outs = call(
            functools.partial(query_back_body, len(going)),
            [sds((width, length), F32), tok_f32] + fold_outs,
            [],
            [dq_flip, cos_flip, sin_flip, kvq, *fold_args],
            flops=2 * length * width * width,
            moved=6000000,
            limit=8,
            name="query_back",
        )
        turned, grad_normed = outs[:2]
        fold_done(going, outs[2:])
        turn = custom and layer == 0
        outs = call(
            functools.partial(kv_back_body, custom, groups, turn),
            blocks_of(width // depths, (width + 2 * kv_width) // parts)
            + [sds((width, length)) if turn else tok_f32, sds((1, width), F32)],
            [idx],
            [
                dkv_sum,
                turned,
                cos_wide,
                sin_wide,
                kvq,
                normed,
                grad_normed,
                entry,
                grad_mid,
                gains[0:1],
            ],
            [
                pltpu.VMEM((2 * kv_width, length), F32),
                pltpu.VMEM((width, length), F32),
                pltpu.VMEM((width, length), BF),
            ],
            flops=4 * length * width * (width + 2 * kv_width),
            moved=5000000,
            after=[result],
            limit=10,
            name="key_value_back",
        )
        c_parts, grad, gain_in = outs[:count], outs[count], outs[count + 1]
        if custom:
            query_sums[layer] = Travelling(*c_parts, True)
        else:
            gate_sums[layer], down_sums[layer] = None, None
            plain = [a_parts[0][0], b_parts[0][0], c_parts[0][0]]
            gate_all, down_all, query_all = plain
            kept[layer] = tuple(
                scatter_plain(v)
                for v in (
                    query_all[:, :width],
                    query_all[:, width : width + kv_width],
                    query_all[:, width + kv_width :],
                    down_all[:, hidden_width:].T,
                    gate_all[:, :hidden_width],
                    gate_all[:, hidden_width:],
                    down_all[:, :hidden_width].T,
                )
            )
        gain_rows[layer] = jnp.concatenate([gain_in, gain_mid])
    gains_here = jnp.concatenate(gain_rows)
    if custom:
        gains = Gains(gains_here)
        gate, down, query = gate_sums, down_sums, query_sums
        step([gate[1], down[1], query[0]], gains, name="sums_one")
        step([gate[0], down[0], query[1]], name="sums_two")
        step([gate[0], down[0], *query, gate[1], down[1]], gains, name="sums_three")
        step([gate[0], down[0], *query], gains, name="sums_four")
        step([query[0]], gains, name="sums_five")
        last = []
        for layer in range(LAYERS):
            for t in (gate[layer], down[layer], query[layer]):
                last += [t.keep, t.got]
        wide = w_query.shape[1]
        *stacked, turned, gain_total = call(
            finish_body,
            [
                sds((LAYERS, wide, width // 8), F32),
                sds((LAYERS, wide, kv_width // 8), F32),
                sds((LAYERS, wide, kv_width // 8), F32),
                sds((LAYERS, wide, width // 8), F32),
                sds((LAYERS, wide, hidden_width // 8), F32),
                sds((LAYERS, wide, hidden_width // 8), F32),
                sds((LAYERS, width // 8, hidden_width // groups), F32),
                sds((2 * LAYERS, width), F32),
            ],
            [],
            last + [gains.value, gains.got],
            limit=8,
            moved=1000000,
            name="finish",
        )
        stacked.append(jnp.swapaxes(turned, 1, 2))
        grad_tokens = relocate(grad).astype(F32).T
    else:
        stacked = [jnp.stack([kept[layer][i] for layer in range(LAYERS)]) for i in range(7)]
        gain_total = lax.psum(gains_here, BOTH)
        grad_tokens = grad
    return (
        result.reshape(sequences, length, width),
        grad_tokens.reshape(sequences, length, width),
        *stacked,
        gain_total.reshape(LAYERS, 2, width),
    )


def solution(mesh):
    sequence = P("replica", "group", None)
    matrix = P(None, "group", None)
    owner = P(None, "group", "replica")
    return jax.shard_map(
        local,
        mesh=mesh,
        in_specs=(sequence, P("replica", "group"), P("replica", "group"), sequence)
        + (matrix,) * 7
        + (P(),),
        out_specs=(sequence, sequence) + (owner,) * 7 + (P(),),
        check_vma=False,
    )
```

```python
import functools

import jax
import jax.numpy as jnp
from jax import lax
from jax.experimental import pallas as pl
from jax.experimental.pallas import tpu as pltpu
from jax.sharding import PartitionSpec as P

QUERY_HEADS = 9
KEY_VALUE_HEADS = 3
HEAD_DIM = 64
LAYERS = 2
EPSILON = 1e-05
MASKED = -1e30
BF = jnp.bfloat16
F32 = jnp.float32
BOTH = ("replica", "group")


def mm(a, b):
    return lax.dot_general(a, b, (((1,), (0,)), ((), ())), preferred_element_type=F32)


def mm_t(a, b):
    return lax.dot_general(a, b, (((1,), (1,)), ((), ())), preferred_element_type=F32)


def flip(value):
    return value.astype(F32).T


def call(
    body, outs, scalars, args, scratch=(), flops=0, moved=0, name=None, after=(), limit=32
):
    vmem = pl.BlockSpec(memory_space=pltpu.VMEM)
    specs = [pl.BlockSpec(memory_space=pltpu.SMEM)] * len(scalars) + [vmem] * len(args)
    specs += [pl.BlockSpec(memory_space=pl.ANY)] * len(after)
    many = isinstance(outs, (list, tuple))
    return pl.pallas_call(
        body,
        out_shape=outs,
        in_specs=specs,
        out_specs=[vmem] * len(outs) if many else vmem,
        scratch_shapes=list(scratch),
        compiler_params=pltpu.CompilerParams(vmem_limit_bytes=limit * 1024 * 1024),
        cost_estimate=pl.CostEstimate(flops=flops, bytes_accessed=moved, transcendentals=0),
        name=name,
    )(*scalars, *args, *after)


def sds(shape, dtype=BF):
    return jax.ShapeDtypeStruct(tuple(shape), dtype)


def rotate(value, cosine, signed_sine):
    lane = lax.broadcasted_iota(jnp.int32, value.shape, 1) % HEAD_DIM
    other = jnp.where(lane < HEAD_DIM // 2, pltpu.roll(value, 96, 1), pltpu.roll(value, 32, 1))
    return value * cosine + other * signed_sine


def qkv_body(x_ref, g_ref, w_ref, cos_ref, sin_ref, n_ref, q_ref, kv_ref):
    x = x_ref[...]
    scale = lax.rsqrt(jnp.mean(x * x, axis=-1, keepdims=True) + EPSILON)
    normed = (x * scale * g_ref[...]).astype(BF)
    n_ref[...] = normed
    raw = mm(normed, w_ref[...])
    cosine, sine = cos_ref[...], sin_ref[...]
    low = lax.broadcasted_iota(jnp.int32, cosine.shape, 1) < HEAD_DIM
    for tile in range(8):
        part = raw[:, 128 * tile : 128 * tile + 128]
        at = slice(128 * tile, 128 * tile + 128)
        if tile == 0:
            kv_ref[:, at] = rotate(part, cosine, sine).astype(BF)
        elif tile == 1:
            kv_ref[:, at] = jnp.where(low, rotate(part, cosine, sine), part).astype(BF)
        elif tile == 2:
            kv_ref[:, at] = part.astype(BF)
        else:
            q_ref[:, 128 * (tile - 3) : 128 * (tile - 2)] = (
                rotate(part, cosine, sine) * 0.125
            ).astype(BF)


def attend_body(pieces, *refs):
    q_ref = refs[0]
    kv_refs = refs[1 : 1 + pieces]
    bias_ref, x_ref, wo_ref, att_ref, lse_ref, mid_ref, k_buf, v_flip, q_flip, att_flip = refs[
        1 + pieces :
    ]
    tokens = q_ref.shape[0]
    half = KEY_VALUE_HEADS * HEAD_DIM
    for p in range(pieces):
        k_buf[p * tokens : (p + 1) * tokens, :] = kv_refs[p][:, :half]
        v_flip[:, p * tokens : (p + 1) * tokens] = flip(kv_refs[p][...])[half:].astype(BF)
    q_flip[...] = flip(q_ref[...]).astype(BF)
    for head in range(QUERY_HEADS):
        group = head // (QUERY_HEADS // KEY_VALUE_HEADS)
        at = slice(HEAD_DIM * head, HEAD_DIM * head + HEAD_DIM)
        kat = slice(HEAD_DIM * group, HEAD_DIM * group + HEAD_DIM)
        scores = mm(k_buf[:, kat], q_flip[at, :]) + bias_ref[...]
        top = jnp.max(scores, axis=0, keepdims=True)
        raised = jnp.exp(scores - top)
        total = jnp.sum(raised, axis=0, keepdims=True)
        out = mm(v_flip[kat, :], raised.astype(BF))
        att_flip[at, :] = out * (1.0 / total)
        lse_ref[head : head + 1, :] = top + jnp.log(total)
    attended = att_flip[...].T.astype(BF)
    att_ref[...] = attended
    mid_ref[...] = x_ref[...] + mm(attended, wo_ref[...])


def ffn_body(mid_ref, g_ref, wgu_ref, wd_ref, out_ref):
    mid = mid_ref[...]
    scale = lax.rsqrt(jnp.mean(mid * mid, axis=-1, keepdims=True) + EPSILON)
    normed = (mid * scale * g_ref[...]).astype(BF)
    gate = mm(normed, wgu_ref[0])
    up = mm(normed, wgu_ref[1])
    hidden = (gate * jax.nn.sigmoid(gate) * up).astype(BF)
    out_ref[...] = (mid + mm(hidden, wd_ref[...])).astype(out_ref.dtype)


def norm_back(value, gain, grad):
    scale = lax.rsqrt(jnp.mean(value * value, axis=-1, keepdims=True) + EPSILON)
    gained = grad * gain
    inner = jnp.mean(gained * value, axis=-1, keepdims=True)
    gain_grad = jnp.sum(grad * value * scale, axis=0, keepdims=True)
    return scale * gained - value * (scale * scale * scale * inner), gain_grad


def slots(custom, x_first):
    if not custom:
        return [(0, 0, None)]
    found = []
    for half in range(2):
        for slot in range(4):
            high, low = slot >> 1, slot & 1
            x_bit, y_bit = (high, low) if x_first else (low, high)
            found.append((half, slot, half + 2 * x_bit + 4 * y_bit))
    return found


def rows_of(idx_ref, xor, rows):
    if xor is None:
        return slice(None)
    return pl.ds(pl.multiple_of((idx_ref[0] ^ xor) * rows, 8), rows)


def by_depth(custom, idx_ref, count, size):
    if not custom:
        return [slice(None)]
    order = [(t & 1) * 2 + (t >> 1) for t in range(count)]
    return [pl.ds(pl.multiple_of((idx_ref[1] ^ t) * size, size & -size), size) for t in order]


def fold(refs, outs):
    for i in range(0, len(refs), 2):
        count = refs[i].shape[0] // 2
        for half in range(2):
            at = slice(half * count, half * count + count)
            total = refs[i][at].astype(F32) + refs[i + 1][at].astype(F32)
            outs[i + half][...] = total.astype(BF)


def step_body(folds, gained, *refs):
    outs = refs[-(2 * folds + gained) :]
    fold(refs[: 2 * folds], outs)
    if gained:
        outs[-1][...] = refs[2 * folds][...] + refs[2 * folds + 1][...]


def ffn_back_body(custom, groups, last, idx_ref, *refs):
    mid_ref, grad_ref, g_ref, gu_ref, wd_ref, wo_ref, att_ref = refs[:7]
    refs = refs[7:]
    count = 2 if custom else 1
    a_refs, b_refs = refs[:count], refs[count : 2 * count]
    gmid_ref, gatt_ref, gain_ref = refs[2 * count : 2 * count + 3]
    refs = refs[2 * count + 3 :]
    if last:
        result_ref, refs = refs[0], refs[1:]
    branch_flip, gate_flip, up_flip, flat, deep_flip, hidden_buf, hidden_deep = refs
    parts = 8 if custom else 1
    depths = groups if custom else 1
    mid, grad = mid_ref[...], grad_ref[...].astype(F32)
    gain = g_ref[...]
    width, hidden_width = branch_flip.shape[0], gate_flip.shape[0]
    cut, hidden_cut = width // depths, hidden_width // depths
    scale = lax.rsqrt(jnp.mean(mid * mid, axis=-1, keepdims=True) + EPSILON)
    normed = (mid * scale * gain).astype(BF)
    gate = mm(normed, gu_ref[0])
    up = mm(normed, gu_ref[1])
    sig = jax.nn.sigmoid(gate)
    hidden_buf[...] = (gate * sig * up).astype(BF)
    if last:
        result_ref[...] = (mid + mm(hidden_buf[...], wd_ref[...])).astype(BF)
    branch = grad.astype(BF)
    branch_flip[...] = flip(branch)
    grad_hidden = mm_t(branch, wd_ref[...])
    grad_gate = (grad_hidden * up * sig * (1.0 + gate * (1.0 - sig))).astype(BF)
    grad_up = (grad_hidden * gate * sig).astype(BF)
    grad_normed = mm_t(grad_gate, gu_ref[0]) + mm_t(grad_up, gu_ref[1])
    back, gain_grad = norm_back(mid, gain, grad_normed)
    grad_mid = grad + back
    gmid_ref[...] = grad_mid
    gain_ref[...] = gain_grad
    attn = grad_mid.astype(BF)
    gatt_ref[...] = mm_t(attn, wo_ref[...]).astype(BF)
    gate_flip[...] = flip(grad_gate).astype(BF)
    up_flip[...] = flip(grad_up).astype(BF)
    flat[...] = flip(normed)
    for t, at in enumerate(by_depth(custom, idx_ref, depths, cut)):
        deep_flip[t * cut : t * cut + cut, :] = flat[at, :].astype(BF)
    rows = hidden_width // parts
    for half, slot, xor in slots(custom, True):
        at = rows_of(idx_ref, xor, rows)
        right = jnp.concatenate([gate_flip[at, :], up_flip[at, :]], axis=0)
        block = mm_t(deep_flip[...], right).astype(BF)
        for t in range(depths):
            a_refs[half][slot * depths + t] = block[t * cut : t * cut + cut]
    for t, at in enumerate(by_depth(custom, idx_ref, depths, hidden_cut)):
        hidden_deep[:, t * hidden_cut : t * hidden_cut + hidden_cut] = hidden_buf[:, at]
    rows = width // parts
    for half, slot, xor in slots(custom, False):
        left = branch_flip[rows_of(idx_ref, xor, rows), :].astype(BF)
        block = mm(left, hidden_deep[...]).astype(BF)
        for t in range(depths):
            b_refs[half][slot * depths + t, :, :hidden_cut] = block[
                :, t * hidden_cut : t * hidden_cut + hidden_cut
            ]
    flat[...] = flip(att_ref[...])
    for t, at in enumerate(by_depth(custom, idx_ref, depths, cut)):
        deep_flip[t * cut : t * cut + cut, :] = flat[at, :].astype(BF)
    branch_flip[...] = flip(attn)
    for half, slot, xor in slots(custom, False):
        left = branch_flip[rows_of(idx_ref, xor, rows), :].astype(BF)
        block = mm_t(left, deep_flip[...]).astype(BF)
        for t in range(depths):
            b_refs[half][slot * depths + t, :, hidden_cut:] = block[:, t * cut : t * cut + cut]


def attend_back_body(pieces, halves, folds, *refs):
    q_ref = refs[0]
    kv_refs = refs[1 : 1 + pieces]
    bias_ref, lse_ref, att_ref, gatt_ref = refs[1 + pieces : 5 + pieces]
    old = refs[5 + pieces : 5 + pieces + 2 * folds]
    refs = refs[5 + pieces + 2 * folds :]
    dq_ref, dkv_refs = refs[0], refs[1 : 1 + halves]
    fold(old, refs[1 + halves : 1 + halves + 2 * folds])
    kv_buf, k_flip, q_flip, g_flip, att_flip, dk_buf, dv_buf = refs[1 + halves + 2 * folds :]
    tokens = q_ref.shape[0]
    half = KEY_VALUE_HEADS * HEAD_DIM
    for p in range(pieces):
        kv_buf[p * tokens : (p + 1) * tokens, :] = kv_refs[p][...]
        k_flip[:, p * tokens : (p + 1) * tokens] = flip(kv_refs[p][...])[:half].astype(BF)
    q_flip[...] = flip(q_ref[...]).astype(BF)
    g_flip[...] = flip(gatt_ref[...]).astype(BF)
    att_flip[...] = flip(att_ref[...])
    per = QUERY_HEADS // KEY_VALUE_HEADS
    for group in range(KEY_VALUE_HEADS):
        kat = slice(HEAD_DIM * group, HEAD_DIM * group + HEAD_DIM)
        vat = slice(half + HEAD_DIM * group, half + HEAD_DIM * group + HEAD_DIM)
        dk = dv = None
        for head in range(per * group, per * group + per):
            at = slice(HEAD_DIM * head, HEAD_DIM * head + HEAD_DIM)
            scores = mm(kv_buf[:, kat], q_flip[at, :]) + bias_ref[...]
            probs = jnp.exp(scores - lse_ref[head : head + 1, :])
            grad_probs = mm(kv_buf[:, vat], g_flip[at, :])
            row_dot = jnp.sum(
                g_flip[at, :].astype(F32) * att_flip[at, :], axis=0, keepdims=True
            )
            grad_scores = (probs * (grad_probs - row_dot)).astype(BF)
            dv_part = mm(probs.astype(BF), gatt_ref[:, at])
            dk_part = mm(grad_scores, q_ref[:, at])
            dv = dv_part if dv is None else dv + dv_part
            dk = dk_part if dk is None else dk + dk_part
            dq_ref[at, :] = mm(k_flip[kat, :], grad_scores) * 0.125
        dk_buf[:, kat] = dk
        dv_buf[:, kat] = dv
    rows = dk_buf.shape[0] // halves
    for h in range(halves):
        at = slice(h * rows, h * rows + rows)
        dkv_refs[h][:, :half] = dk_buf[at, :].astype(BF)
        dkv_refs[h][:, half:] = dv_buf[at, :].astype(BF)


def query_back_body(folds, dq_ref, cos_ref, sin_ref, w_ref, *refs):
    old = refs[: 2 * folds]
    turned, gn_ref = refs[2 * folds : 2 * folds + 2]
    fold(old, refs[2 * folds + 2 :])
    cosine, sine = cos_ref[...], sin_ref[...]
    mid = HEAD_DIM // 2
    for head in range(QUERY_HEADS):
        a = dq_ref[HEAD_DIM * head : HEAD_DIM * head + mid, :]
        b = dq_ref[HEAD_DIM * head + mid : HEAD_DIM * head + HEAD_DIM, :]
        turned[HEAD_DIM * head : HEAD_DIM * head + mid, :] = a * cosine + b * sine
        turned[HEAD_DIM * head + mid : HEAD_DIM * head + HEAD_DIM, :] = b * cosine - a * sine
    width = turned.shape[0]
    grad_query = turned[...].T.astype(BF)
    kv_width = 2 * KEY_VALUE_HEADS * HEAD_DIM
    gn_ref[...] = mm_t(grad_query, w_ref[:, kv_width : kv_width + width])


def kv_back_body(custom, groups, turn, idx_ref, *refs):
    dkv_ref, turned, cos_ref, sin_ref, w_ref, n_ref, gn_ref, x_ref, gmid_ref, g_ref = refs[:10]
    refs = refs[11:]
    count = 2 if custom else 1
    c_refs = refs[:count]
    grad_ref, gain_ref, kv_flip, flat, deep_flip = refs[count:]
    parts = 8 if custom else 1
    depths = groups if custom else 1
    dkv = dkv_ref[...]
    cosine, sine = cos_ref[...], -sin_ref[...]
    low = lax.broadcasted_iota(jnp.int32, cosine.shape, 1) < HEAD_DIM
    first = rotate(dkv[:, :128], cosine, sine)
    second = jnp.where(low, rotate(dkv[:, 128:256], cosine, sine), dkv[:, 128:256])
    grad_kv = jnp.concatenate([first, second, dkv[:, 256:]], axis=1)
    kv_flip[...] = grad_kv.T
    normed = n_ref[...]
    kv_width, width = KEY_VALUE_HEADS * HEAD_DIM, turned.shape[0]
    cut = width // depths
    grad_normed = gn_ref[...] + mm_t(grad_kv.astype(BF), w_ref[:, : 2 * kv_width])
    back, gain_grad = norm_back(x_ref[...], g_ref[...], grad_normed)
    grad = gmid_ref[...] + back
    grad_ref[...] = (grad.T if turn else grad).astype(grad_ref.dtype)
    gain_ref[...] = gain_grad
    flat[...] = flip(normed)
    for t, at in enumerate(by_depth(custom, idx_ref, depths, cut)):
        deep_flip[t * cut : t * cut + cut, :] = flat[at, :].astype(BF)
    rows = kv_width // parts
    for half, slot, xor in slots(custom, True):
        if xor is None:
            right = jnp.concatenate([turned[...], kv_flip[...]], axis=0)
        else:
            start = pl.multiple_of((idx_ref[0] ^ xor) * rows, 8)
            right = jnp.concatenate(
                [
                    turned[rows_of(idx_ref, xor, width // parts), :],
                    kv_flip[pl.ds(start, rows), :],
                    kv_flip[pl.ds(kv_width + start, rows), :],
                ],
                axis=0,
            )
        block = mm_t(deep_flip[...], right.astype(BF)).astype(BF)
        for t in range(depths):
            c_refs[half][slot * depths + t] = block[t * cut : t * cut + cut]


def finish_body(*refs):
    parts, gain_ref, came_ref = refs[:12], refs[12], refs[13]
    gq_ref, gk_ref, gv_ref, go_ref, gg_ref, gu_ref, gd_ref, total_ref = refs[14:]
    total_ref[...] = gain_ref[...] + came_ref[...]
    for layer in range(LAYERS):
        total = [
            parts[6 * layer + 2 * i][0].astype(F32) + parts[6 * layer + 2 * i + 1][0].astype(F32)
            for i in range(3)
        ]
        gate_width, rows = gg_ref.shape[2], gd_ref.shape[2]
        gg_ref[layer] = total[0][:, :gate_width]
        gu_ref[layer] = total[0][:, gate_width:]
        gd_ref[layer] = total[1][:, :rows]
        go_ref[layer] = total[1][:, rows:].T
        q_width, k_width = gq_ref.shape[2], gk_ref.shape[2]
        gq_ref[layer] = total[2][:, :q_width]
        gk_ref[layer] = total[2][:, q_width : q_width + k_width]
        gv_ref[layer] = total[2][:, q_width + k_width :]


def attention_unit(layer, wk_ref, wv_ref, wq_ref, wo_ref):
    return jnp.concatenate(
        [wk_ref[layer], wv_ref[layer], wq_ref[layer], wo_ref[layer]], axis=1
    )


def columns_of(idx_ref, width):
    return pl.ds(pl.multiple_of((idx_ref[0] >> 1) * width, 128), width)


def first_pieces_body(idx_ref, wk_ref, wv_ref, wq_ref, wo_ref, unit_ref, piece_ref):
    unit_ref[...] = attention_unit(0, wk_ref, wv_ref, wq_ref, wo_ref)
    rows, cols = piece_ref.shape
    start = pl.multiple_of((idx_ref[0] & 1) * (unit_ref.shape[0] - rows), 16)
    piece_ref[...] = unit_ref[pl.ds(start, rows), columns_of(idx_ref, cols)]


def stack_into(refs, out_ref):
    for i, ref in enumerate(refs):
        out_ref[i] = ref[...]


def put_gate_piece(idx_ref, layer, wg_ref, wu_ref, out_ref):
    rows = wg_ref.shape[1]
    at = columns_of(idx_ref, out_ref.shape[1])

    @pl.when((idx_ref[0] & 1) == 0)
    def _():
        out_ref[:rows, :] = wg_ref[layer, :, at]

    @pl.when((idx_ref[0] & 1) == 1)
    def _():
        out_ref[:rows, :] = wu_ref[layer, :, at]


def put_down_piece(idx_ref, layer, wd_ref, out_ref, base):
    cols = out_ref.shape[1]
    own = wd_ref.shape[1] // 8
    down = wd_ref[layer, pl.ds(pl.multiple_of(idx_ref[0] * own, 16), own), :].astype(F32)
    rest = down[:, cols:]
    out_ref[base : base + own, :] = down[:, :cols].astype(BF)
    out_ref[base + own :, :] = jnp.concatenate(
        [rest[: own // 2], rest[own // 2 :]], axis=1
    ).astype(BF)


def ffn_piece_body(count, idx_ref, *refs):
    column_out, piece_ref = refs[-2:]
    stack_into(refs[:count], column_out)
    wg_ref, wu_ref, wd_ref = refs[count : count + 3]
    put_gate_piece(idx_ref, 0, wg_ref, wu_ref, piece_ref)
    put_down_piece(idx_ref, 0, wd_ref, piece_ref, wg_ref.shape[1])


def second_pieces_body(count, idx_ref, *refs):
    column_out, unit_ref, attention_ref, gate_ref = refs[-4:]
    stack_into(refs[:count], column_out)
    wk_ref, wv_ref, wq_ref, wo_ref, wg_ref, wu_ref, wd_ref = refs[count : count + 7]
    unit_ref[...] = attention_unit(1, wk_ref, wv_ref, wq_ref, wo_ref)
    height = wg_ref.shape[1] - 64
    start = pl.multiple_of((idx_ref[0] & 1) * 64, 16)
    attention_ref[:height, :] = unit_ref[
        pl.ds(start, height), columns_of(idx_ref, attention_ref.shape[1])
    ]
    put_down_piece(idx_ref, 1, wd_ref, attention_ref, height)
    put_gate_piece(idx_ref, 1, wg_ref, wu_ref, gate_ref)


def stack_body(count, *refs):
    stack_into(refs[:count], refs[-1])


def place_all(refs, idx_ref, x_first, group_size, put):
    for combo, ref in enumerate(refs):
        s_bit, c_bit = combo & 1, combo >> 1
        core = (idx_ref[0] & 1) ^ c_bit
        for f_bit in range(2):
            chip = (idx_ref[0] >> 1) ^ ((f_bit + 2 * s_bit) if x_first else (2 * f_bit + s_bit))
            for k in range(group_size - 1):
                depth = lax.rem(idx_ref[1] - (k + 1) + group_size, group_size)
                put(chip, depth, core, ref, f_bit, k)


def put_attention(buf, rows, cols, chip, depth, core, piece):
    at = pl.multiple_of(depth * rows + core * (rows - piece.shape[0]), 16)
    buf[pl.ds(at, piece.shape[0]), pl.ds(pl.multiple_of(chip * (cols // 4), 128), cols // 4)] = piece


def finish_attention(buf, idx_ref, unit_ref, kvq_ref, o_ref):
    rows, cols = unit_ref.shape
    buf[pl.ds(pl.multiple_of(idx_ref[1] * rows, 16), rows), :] = unit_ref[...]
    used = cols - o_ref.shape[1]
    kvq_ref[:, used // 128 * 128 :] = jnp.zeros_like(kvq_ref[:, used // 128 * 128 :])
    kvq_ref[:, :used] = buf[:, :used]
    o_ref[...] = buf[:, used:]


def put_gate(gu_ref, rows, chip, depth, core, piece):
    gu_ref[
        core,
        pl.ds(pl.multiple_of(depth * rows, 16), rows),
        pl.ds(pl.multiple_of(chip * piece.shape[1], 128), piece.shape[1]),
    ] = piece


def put_down(down_ref, rows, chip, depth, core, piece):
    own = rows // 8
    cols = piece.shape[1]
    at = pl.multiple_of(depth * rows + (2 * chip + core) * own, 16)
    down_ref[pl.ds(at, own), :cols] = piece[:own]
    rest = piece[own:].astype(F32)
    wide = down_ref.shape[1] - cols
    down_ref[pl.ds(at, own), cols:] = jnp.concatenate(
        [rest[:, :wide], rest[:, wide:]], axis=0
    ).astype(BF)


def finish_gate(layer, idx_ref, wg_ref, wu_ref, gu_ref):
    rows = wg_ref.shape[1]
    own = pl.ds(pl.multiple_of(idx_ref[1] * rows, 16), rows)
    gu_ref[0, own, :] = wg_ref[layer]
    gu_ref[1, own, :] = wu_ref[layer]


def finish_down(layer, idx_ref, wd_ref, down_ref):
    rows = wd_ref.shape[1]
    down_ref[pl.ds(pl.multiple_of(idx_ref[1] * rows, 16), rows), :] = wd_ref[layer]


def place_first_body(x_first, groups, idx_ref, unit_ref, *refs):
    kvq_ref, o_ref, buf = refs[4:]
    rows, cols = unit_ref.shape

    def put(chip, depth, core, ref, f_bit, k):
        put_attention(buf, rows, cols, chip, depth, core, ref[f_bit, k])

    place_all(refs[:4], idx_ref, x_first, groups, put)
    finish_attention(buf, idx_ref, unit_ref, kvq_ref, o_ref)


def place_ffn_body(x_first, groups, idx_ref, wg_ref, wu_ref, wd_ref, *refs):
    gu_ref, down_ref = refs[4:]
    rows = wg_ref.shape[1]

    def put(chip, depth, core, ref, f_bit, k):
        put_gate(gu_ref, rows, chip, depth, core, ref[f_bit, k, :rows, :])
        put_down(down_ref, wd_ref.shape[1], chip, depth, core, ref[f_bit, k, rows:, :])

    place_all(refs[:4], idx_ref, x_first, groups, put)
    finish_gate(0, idx_ref, wg_ref, wu_ref, gu_ref)
    finish_down(0, idx_ref, wd_ref, down_ref)


def place_second_body(x_first, groups, idx_ref, unit_ref, wd_ref, *refs):
    kvq_ref, o_ref, down_ref, buf = refs[4:]
    rows, cols = unit_ref.shape
    height = rows - 64

    def put(chip, depth, core, ref, f_bit, k):
        put_attention(buf, rows, cols, chip, depth, core, ref[f_bit, k, :height, :])
        put_down(down_ref, wd_ref.shape[1], chip, depth, core, ref[f_bit, k, height:, :])

    place_all(refs[:4], idx_ref, x_first, groups, put)
    finish_attention(buf, idx_ref, unit_ref, kvq_ref, o_ref)
    finish_down(1, idx_ref, wd_ref, down_ref)


def place_gate_body(x_first, groups, idx_ref, wg_ref, wu_ref, *refs):
    gu_ref = refs[4]
    rows = wg_ref.shape[1]

    def put(chip, depth, core, ref, f_bit, k):
        put_gate(gu_ref, rows, chip, depth, core, ref[f_bit, k])

    place_all(refs[:4], idx_ref, x_first, groups, put)
    finish_gate(1, idx_ref, wg_ref, wu_ref, gu_ref)


def xor_pairs(count, bits):
    return [(i, i ^ bits) for i in range(count)]


def swap(value, bits):
    return lax.ppermute(value, "replica", xor_pairs(lax.axis_size("replica"), bits))


def swap_deep(value, bits):
    return lax.ppermute(value, "group", xor_pairs(lax.axis_size("group"), bits))


def from_column(piece):
    groups = lax.axis_size("group")
    return [
        lax.ppermute(piece, "group", [(i, (i + k) % groups) for i in range(groups)])
        for k in range(1, groups)
    ]


def stacked_after(parts, after, name):
    return call(
        functools.partial(stack_body, len(parts)),
        sds((len(parts),) + parts[0].shape),
        [],
        parts,
        after=after,
        limit=4,
        moved=1000000,
        name=name,
    )


def to_all(pair, bits):
    other = swap(pair, bits)
    return pair, other, swap(pair, 1), swap(other, 1)


def gather(value):
    return lax.all_gather(value, "group", axis=0, tiled=True)


def plain_weights(layer, wq, wk, wv, wo, wg, wu, wd):
    pad = jnp.zeros((wq.shape[1], 64), BF)
    return (
        gather(jnp.concatenate([wk[layer], wv[layer], wq[layer], pad], axis=1)),
        gather(wo[layer]),
        jnp.stack([gather(wg[layer]), gather(wu[layer])]),
        gather(wd[layer]),
    )


class Weights:
    def __init__(self, idx, wq, wk, wv, wo, wg, wu, wd):
        self.idx, self.four, self.ffn = idx, [wk, wv, wq, wo], [wg, wu, wd]
        self.groups = lax.axis_size("group")
        self.rows, self.ff = wg.shape[1:]
        self.cols, self.width = self.ff // 4, wo.shape[2]
        self.down_rows = wd.shape[1]
        self.down = wd.shape[1] // 8 * self.width // self.cols
        count = self.groups - 1
        unit, piece = call(
            first_pieces_body,
            [sds((self.rows, self.ff)), sds((self.rows - 64, self.cols))],
            [idx],
            self.four,
            limit=8,
            moved=1000000,
            name="first_pieces",
        )
        column, ffn_piece = call(
            functools.partial(ffn_piece_body, count),
            [sds((count, self.rows - 64, self.cols)), sds((self.rows + self.down, self.cols))],
            [idx],
            [*from_column(piece), *self.ffn],
            limit=8,
            moved=2000000,
            name="ffn_piece",
        )
        self.ffn_column = from_column(ffn_piece)
        pair = stacked_after([column, swap(column, 2)], [], "first_pair")
        arrived = to_all(pair, 4)
        self.first = call(
            functools.partial(place_first_body, True, self.groups),
            self.attention_shapes(),
            [idx],
            [unit, *arrived],
            [pltpu.VMEM((self.rows * self.groups, self.ff), BF)],
            limit=12,
            moved=4000000,
            name="place_first",
        )
        height = self.rows - 64 + self.down
        column, self.unit, attention_piece, gate_piece = call(
            functools.partial(second_pieces_body, count),
            [
                sds((count, self.rows + self.down, self.cols)),
                sds((self.rows, self.ff)),
                sds((height, self.cols)),
                sds((self.rows, self.cols)),
            ],
            [idx],
            [*self.ffn_column, *self.four, *self.ffn],
            after=[arrived[1]],
            limit=8,
            moved=4000000,
            name="second_pieces",
        )
        self.ffn_parts = [column, swap(column, 4)]
        self.second_column = from_column(attention_piece)
        self.gate_piece = gate_piece

    def attention_shapes(self):
        full = self.rows * self.groups
        return [sds((full, 1024)), sds((full, self.width))]

    def gate_shape(self):
        return sds((2, self.rows * self.groups, self.ff))

    def down_shape(self):
        return sds((self.down_rows * self.groups, self.width))

    def after_project(self, token):
        pair = stacked_after(self.ffn_parts, [token], "ffn_pair")
        column = stacked_after(self.second_column, [pair], "second_column")
        self.gate_column = from_column(self.gate_piece)
        self.ffn_arrived = to_all(pair, 2)
        self.second_parts = [column, swap(column, 2)]

    def after_attend(self, token):
        pair = stacked_after(self.second_parts, [token], "second_pair")
        self.second_arrived = to_all(pair, 4)
        column = stacked_after(self.gate_column, [pair], "gate_column")
        self.gate_parts = [column, swap(column, 4)]

    def feed_forward(self):
        return call(
            functools.partial(place_ffn_body, False, self.groups),
            [self.gate_shape(), self.down_shape()],
            [self.idx],
            [*self.ffn, *self.ffn_arrived],
            limit=8,
            moved=10000000,
            name="place_ffn",
        )

    def after_feed_forward(self, token):
        pair = stacked_after(self.gate_parts, [token], "gate_pair")
        self.gate_arrived = to_all(pair, 2)

    def second(self):
        return call(
            functools.partial(place_second_body, True, self.groups),
            self.attention_shapes() + [self.down_shape()],
            [self.idx],
            [self.unit, self.ffn[2], *self.second_arrived],
            [pltpu.VMEM((self.rows * self.groups, self.ff), BF)],
            limit=8,
            moved=8000000,
            name="place_second",
        )

    def gate(self):
        return call(
            functools.partial(place_gate_body, False, self.groups),
            self.gate_shape(),
            [self.idx],
            [*self.ffn[:2], *self.gate_arrived],
            limit=8,
            moved=7000000,
            name="place_gate",
        )


def plus(a, b):
    return (a.astype(F32) + b.astype(F32)).astype(BF)


class Travelling:
    def __init__(self, keep, send, x_first):
        first, second = (2, 4) if x_first else (4, 2)
        self.steps = [(swap, 1), (swap, first), (swap, second), (swap_deep, 1), (swap_deep, 2)]
        self.keep, self.send = keep, send
        self.go()

    def go(self):
        way, bits = self.steps.pop(0)
        self.got = way(self.send, bits)

    def folded(self, low, high):
        self.keep, self.send = low, high
        self.go()


class Gains:
    def __init__(self, value):
        self.steps = [(swap, 1), (swap, 2), (swap, 4), (swap_deep, 1), (swap_deep, 2)]
        self.go(value)

    def go(self, value):
        way, bits = self.steps.pop(0)
        self.value, self.got = value, way(value, bits)


def step(travellers, gains=None, name=None, after=()):
    args, outs = fold_with(travellers)
    if gains is not None:
        args = args + [gains.value, gains.got]
        outs = outs + [sds(gains.value.shape, F32)]
    results = call(
        functools.partial(step_body, len(travellers), gains is not None),
        outs,
        [],
        args,
        after=after,
        limit=8,
        moved=2000000,
        name=name,
    )
    fold_done(travellers, results)
    if gains is not None:
        gains.go(results[-1])


def fold_with(travellers):
    args, outs = [], []
    for t in travellers:
        shape = (t.keep.shape[0] // 2,) + t.keep.shape[1:]
        args += [t.keep, t.got]
        outs += [sds(shape), sds(shape)]
    return args, outs


def fold_done(travellers, results):
    for i, t in enumerate(travellers):
        t.folded(results[2 * i], results[2 * i + 1])


def scatter_plain(value):
    part = lax.psum_scatter(value, "replica", scatter_dimension=1, tiled=True)
    return lax.psum_scatter(part, "group", scatter_dimension=0, tiled=True).astype(F32)


def local(
    tokens,
    segments,
    positions,
    cotangent,
    w_query,
    key_weight,
    value_weight,
    w_out,
    w_gate,
    w_up,
    w_down,
    norm_gains,
):
    sequences, length, width = tokens.shape
    replicas, groups = lax.axis_size("replica"), lax.axis_size("group")
    r, z = lax.axis_index("replica"), lax.axis_index("group")
    custom = replicas == 8 and groups == 4
    idx = jnp.stack([r, z]).astype(jnp.int32)
    hidden_width = w_gate.shape[2]
    kv_width = key_weight.shape[2]
    full = length * groups
    core_pairs = xor_pairs(replicas, 1)
    z_pairs = xor_pairs(groups, 1)

    half_way = groups // 2
    exchange = []
    for i in range(replicas):
        for j in range(groups):
            if i % 2 == 1 and j < half_way:
                target = (i - 1, j + half_way)
            elif i % 2 == 0 and j >= half_way:
                target = (i + 1, j - half_way)
            else:
                target = (i, j)
            exchange.append((i * groups + j, target[0] * groups + target[1]))

    def relocate(value):
        return lax.ppermute(value, BOTH, exchange) if custom else value

    def share(value):
        if not custom:
            every = lax.all_gather(value, "group", axis=0, tiled=False)
            return [every[i] for i in range(groups)]
        deep = lax.ppermute(value, "group", z_pairs)
        return [
            value,
            deep,
            lax.ppermute(value, "replica", core_pairs),
            lax.ppermute(deep, "replica", core_pairs),
        ]

    tokens = relocate(tokens.reshape(length, width))
    labels = relocate(jnp.stack([segments.reshape(length), positions.reshape(length)]))
    cotangent = relocate(cotangent.reshape(length, width))
    seg, pos = labels[0], labels[1]
    seg_all = jnp.concatenate(share(seg))
    if custom:
        block_at = lambda c, zz: c * half_way + zz % half_way
        c = r & 1
        blocks = [
            block_at(c, z),
            block_at(c, z ^ 1),
            block_at(c ^ 1, z),
            block_at(c ^ 1, z ^ 1),
        ]
    else:
        blocks = list(range(groups))
    mine_block = blocks[0] if custom else z
    ramp = jnp.arange(length, dtype=jnp.int32)
    place_all_keys = jnp.concatenate([b * length + ramp for b in blocks])
    place = mine_block * length + ramp
    allowed = (seg_all[:, None] == seg[None, :]) & (place_all_keys[:, None] <= place[None, :])
    bias = jnp.where(allowed, 0.0, MASKED).astype(F32)

    half_head = HEAD_DIM // 2
    inverse_freq = jnp.power(
        10000.0, -jnp.arange(half_head, dtype=F32) * (2.0 / HEAD_DIM)
    )
    angles = pos.astype(F32)[:, None] * inverse_freq
    cosine, sine = jnp.cos(angles), jnp.sin(angles)
    cos_wide = jnp.concatenate([cosine] * 4, axis=1)
    sin_wide = jnp.concatenate([-sine, sine] * 2, axis=1)
    cos_flip, sin_flip = cosine.T, sine.T

    matrices = (w_query, key_weight, value_weight, w_out, w_gate, w_up, w_down)
    if custom:
        moving = Weights(idx, *matrices)
        weights = [None] * LAYERS
    else:
        weights = [plain_weights(layer, *matrices) for layer in range(LAYERS)]

    tok_f32 = sds((length, width), F32)
    stream = tokens.astype(F32)
    kept = []
    att_flops = 4 * QUERY_HEADS * HEAD_DIM * length * full
    ffn_flops = 6 * length * width * hidden_width
    for layer in range(LAYERS):
        gains = norm_gains[layer]
        if not custom:
            kvq, wo, gu, down = weights[layer]
        elif layer == 0:
            kvq, wo = moving.first
        else:
            kvq, wo, down = moving.second()
        normed, q, kv = call(
            qkv_body,
            [sds((length, width)), sds((length, 640)), sds((length, 2 * kv_width))],
            [],
            [stream, gains[0:1], kvq, cos_wide, sin_wide],
            flops=2 * length * width * 1024,
            moved=2000000,
            limit=12,
            name="project",
        )
        pieces = share(kv)
        if custom and layer == 0:
            moving.after_project(q)
        attended, lse, middle = call(
            functools.partial(attend_body, groups),
            [sds((length, width)), sds((16, length), F32), tok_f32],
            [],
            [q, *pieces, bias, stream, wo],
            [
                pltpu.VMEM((full, kv_width), BF),
                pltpu.VMEM((kv_width, full), BF),
                pltpu.VMEM((640, length), BF),
                pltpu.VMEM((width, length), F32),
            ],
            flops=4 * att_flops,
            moved=4000000,
            limit=16,
            name="attend",
        )
        if custom and layer == 0:
            moving.after_attend(middle)
            gu, down = moving.feed_forward()
        elif custom:
            gu = moving.gate()
        weights[layer] = (kvq, wo, gu, down)
        kept.append((stream, normed, q, pieces, lse, attended, middle))
        if layer + 1 < LAYERS:
            stream = call(
                ffn_body,
                tok_f32,
                [],
                [middle, gains[1:2], gu, down],
                flops=ffn_flops,
                moved=7000000,
                limit=16,
                name="feed_forward",
            )
            if custom:
                moving.after_feed_forward(stream)

    grad = cotangent
    parts = 8 if custom else 1
    count = 2 if custom else 1
    depths = groups if custom else 1
    blocks_here = parts // count * depths
    gain_rows = [None] * LAYERS
    gate_sums, down_sums, query_sums = [None] * LAYERS, [None] * LAYERS, [None] * LAYERS
    for layer in reversed(range(LAYERS)):
        kvq, wo, gu, down = weights[layer]
        entry, normed, q, pieces, lse, attended, middle = kept[layer]
        gains = norm_gains[layer]

        def blocks_of(rows, cols):
            return [sds((blocks_here, rows, cols))] * count

        last = layer + 1 == LAYERS
        outs = call(
            functools.partial(ffn_back_body, custom, groups, last),
            blocks_of(width // depths, 2 * hidden_width // parts)
            + blocks_of(width // parts, (hidden_width + width) // depths)
            + [tok_f32, sds((length, width)), sds((1, width), F32)]
            + [sds((length, width))] * last,
            [idx],
            [middle, grad, gains[1:2], gu, down, wo, attended],
            [
                pltpu.VMEM((width, length), F32),
                pltpu.VMEM((hidden_width, length), BF),
                pltpu.VMEM((hidden_width, length), BF),
                pltpu.VMEM((width, length), F32),
                pltpu.VMEM((width, length), BF),
                pltpu.VMEM((length, hidden_width), BF),
                pltpu.VMEM((length, hidden_width), BF),
            ],
            flops=3 * ffn_flops,
            moved=16000000,
            limit=24,
            name="feed_forward_back",
        )
        a_parts, b_parts = outs[:count], outs[count : 2 * count]
        grad_mid, grad_att, gain_mid = outs[2 * count : 2 * count + 3]
        if last:
            result = relocate(outs[2 * count + 3])
        if custom:
            gate_sums[layer] = Travelling(*a_parts, True)
            down_sums[layer] = Travelling(*b_parts, False)
        halves = 2 if custom else 1
        above = [gate_sums[1], down_sums[1]] if custom and layer == 0 else []
        fold_args, fold_outs = fold_with(above)
        outs = call(
            functools.partial(attend_back_body, groups, halves, len(above)),
            [sds((width, length), F32)]
            + [sds((full // halves, 2 * kv_width))] * halves
            + fold_outs,
            [],
            [q, *pieces, bias, lse, attended, grad_att, *fold_args],
            [
                pltpu.VMEM((full, 2 * kv_width), BF),
                pltpu.VMEM((kv_width, full), BF),
                pltpu.VMEM((640, length), BF),
                pltpu.VMEM((width, length), BF),
                pltpu.VMEM((width, length), F32),
                pltpu.VMEM((full, kv_width), F32),
                pltpu.VMEM((full, kv_width), F32),
            ],
            flops=10 * att_flops,
            moved=6000000,
            limit=20,
            name="attend_back",
        )
        dq_flip, dkv = outs[0], outs[1 : 1 + halves]
        fold_done(above, outs[1 + halves :])
        if custom:
            got = swap(dkv[1], 1)
            deep = plus(dkv[0][length:], got[length:])
            near = dkv[0][:length].astype(F32) + got[:length].astype(F32)
            dkv_sum = near + swap_deep(deep, 1).astype(F32)
        else:
            dkv_sum = lax.psum_scatter(dkv[0], "group", scatter_dimension=0, tiled=True).astype(F32)
        going = [gate_sums[layer], down_sums[layer], query_sums[1]] if custom else []
        going = [t for t in going if t is not None]
        fold_args, fold_outs = fold_with(going)
        outs = call(
            functools.partial(query_back_body, len(going)),
            [sds((width, length), F32), tok_f32] + fold_outs,
            [],
            [dq_flip, cos_flip, sin_flip, kvq, *fold_args],
            flops=2 * length * width * width,
            moved=6000000,
            limit=8,
            name="query_back",
        )
        turned, grad_normed = outs[:2]
        fold_done(going, outs[2:])
        turn = custom and layer == 0
        outs = call(
            functools.partial(kv_back_body, custom, groups, turn),
            blocks_of(width // depths, (width + 2 * kv_width) // parts)
            + [sds((width, length)) if turn else tok_f32, sds((1, width), F32)],
            [idx],
            [
                dkv_sum,
                turned,
                cos_wide,
                sin_wide,
                kvq,
                normed,
                grad_normed,
                entry,
                grad_mid,
                gains[0:1],
            ],
            [
                pltpu.VMEM((2 * kv_width, length), F32),
                pltpu.VMEM((width, length), F32),
                pltpu.VMEM((width, length), BF),
            ],
            flops=4 * length * width * (width + 2 * kv_width),
            moved=5000000,
            after=[result],
            limit=10,
            name="key_value_back",
        )
        c_parts, grad, gain_in = outs[:count], outs[count], outs[count + 1]
        if custom:
            query_sums[layer] = Travelling(*c_parts, True)
        else:
            gate_sums[layer], down_sums[layer] = None, None
            plain = [a_parts[0][0], b_parts[0][0], c_parts[0][0]]
            gate_all, down_all, query_all = plain
            kept[layer] = tuple(
                scatter_plain(v)
                for v in (
                    query_all[:, :width],
                    query_all[:, width : width + kv_width],
                    query_all[:, width + kv_width :],
                    down_all[:, hidden_width:].T,
                    gate_all[:, :hidden_width],
                    gate_all[:, hidden_width:],
                    down_all[:, :hidden_width].T,
                )
            )
        gain_rows[layer] = jnp.concatenate([gain_in, gain_mid])
    gains_here = jnp.concatenate(gain_rows)
    if custom:
        gains = Gains(gains_here)
        gate, down, query = gate_sums, down_sums, query_sums
        step([gate[1], down[1], query[0]], gains, name="sums_one")
        step([gate[0], down[0], query[1]], name="sums_two")
        step([gate[0], down[0], *query, gate[1], down[1]], gains, name="sums_three")
        step([gate[0], down[0], *query], gains, name="sums_four")
        placed = relocate(grad)
        step([query[0]], gains, name="sums_five", after=[placed])
        last = []
        for layer in range(LAYERS):
            for t in (gate[layer], down[layer], query[layer]):
                last += [t.keep, t.got]
        wide = w_query.shape[1]
        *stacked, turned, gain_total = call(
            finish_body,
            [
                sds((LAYERS, wide, width // 8), F32),
                sds((LAYERS, wide, kv_width // 8), F32),
                sds((LAYERS, wide, kv_width // 8), F32),
                sds((LAYERS, wide, width // 8), F32),
                sds((LAYERS, wide, hidden_width // 8), F32),
                sds((LAYERS, wide, hidden_width // 8), F32),
                sds((LAYERS, width // 8, hidden_width // groups), F32),
                sds((2 * LAYERS, width), F32),
            ],
            [],
            last + [gains.value, gains.got],
            limit=8,
            moved=1000000,
            name="finish",
        )
        stacked.append(jnp.swapaxes(turned, 1, 2))
        grad_tokens = placed.astype(F32).T
    else:
        stacked = [jnp.stack([kept[layer][i] for layer in range(LAYERS)]) for i in range(7)]
        gain_total = lax.psum(gains_here, BOTH)
        grad_tokens = grad
    return (
        result.reshape(sequences, length, width),
        grad_tokens.reshape(sequences, length, width),
        *stacked,
        gain_total.reshape(LAYERS, 2, width),
    )


def solution(mesh):
    sequence = P("replica", "group", None)
    matrix = P(None, "group", None)
    owner = P(None, "group", "replica")
    return jax.shard_map(
        local,
        mesh=mesh,
        in_specs=(sequence, P("replica", "group"), P("replica", "group"), sequence)
        + (matrix,) * 7
        + (P(),),
        out_specs=(sequence, sequence) + (owner,) * 7 + (P(),),
        check_vma=False,
    )
```
